128 devices in a mesh: leaf: 32 (over y, z, core), panel: 4 (over x).
Axes of the slice: x: 4, y: 4, z: 4, core: 2. Of those that a mesh axis runs over, the one named last changes fastest.
Arguments:
- noise_parts: float32 [131072, 128], P(('leaf', 'panel')), may hold values from -6 to 6
- elimination_row: int32 [131072], P(('leaf', 'panel')), may hold values from 0 to 131071, as said below
- leaf_noise: float32 [524288, 128], P(('leaf', 'panel')), may hold values from -6 to 6
- diag_inverse: float32 [5120, 128, 128], P(('leaf', 'panel')), as said below
- panels: bfloat16 [71680, 128, 128], P(('leaf', 'panel')), may hold values from -0.125 to 0.125
- panel_from: int32 [71680], P(('leaf', 'panel')), may hold values from 0 to 127, as said below
- send_lists: int32 [128, 240], P(('leaf', 'panel')), may hold values from 0 to 1
Outputs:
- sep_solution: float32 [131072, 128], P(('leaf', 'panel'))
- leaf_solution: float32 [524288, 128], P(('leaf', 'panel'))
The draws below stay inside these ranges and needn't reach their ends.
Inputs may be any that keep to these rules, and one draw needn't show every extreme that they name: `elimination_row`: A permutation of the separator rows in which every device hands exactly 8 rows to every device. `panel_from`: the block of ancestor level l names only positions below 128 / 2^l, and every one of them at least once. `diag_inverse`: each tile is upper triangular with diagonal entries between 0.6 and 1.4.
All inputs are finite; a program needn't handle non-finite values.
Results may differ from the reference program's by a relative error of at most 0.0029.
Values may be sent and summed in bfloat16 or wider, within the bound.
No kernel may reach another device: no remote copies, remote signals or barrier semaphores. Data moves between devices by JAX's collectives and lax.ppermute only.
A program may use at most 128 MiB of HBM per device.

```python
import jax
import jax.numpy as jnp
from jax import lax

BS = 128
RHS = 128
TS = 2
TL = 32
KP = 4
LEVELS = 4
OWNER_DEVICES = 128
DEVICE_SEP_ROWS = 1024
SEPARATOR_ROWS = 131072
PER_PEER = 8
NTILES = 40
NPAN = 560
SENDS = 240


def draw_elimination_row(key, part):
    key = jax.random.fold_in(key, 11)
    first_key, second_key = jax.random.split(key)
    local_slot_ordering = jax.vmap(lambda device: jax.random.permutation(jax.random.fold_in(first_key, device), DEVICE_SEP_ROWS))(jnp.arange(OWNER_DEVICES))
    local_slot_ordering = local_slot_ordering.reshape(OWNER_DEVICES, OWNER_DEVICES, PER_PEER)
    eliminated_rows = jnp.arange(OWNER_DEVICES, dtype=jnp.int32)[:, None, None] * DEVICE_SEP_ROWS + local_slot_ordering
    grouped_by_sender = jnp.transpose(eliminated_rows, (1, 0, 2)).reshape(OWNER_DEVICES, DEVICE_SEP_ROWS)
    shuffled = jax.vmap(lambda row_block, device: jax.random.permutation(jax.random.fold_in(second_key, device), row_block))(grouped_by_sender, jnp.arange(OWNER_DEVICES))
    return shuffled.reshape(-1).astype(jnp.int32)


def draw_diag_inverse(key, part):
    key = jax.random.fold_in(key, 5)
    first_key, second_key = jax.random.split(key)
    shape = (OWNER_DEVICES * NTILES, BS, BS)
    diagonal = jax.random.uniform(first_key, shape, jnp.float32, 0.6, 1.4)
    upper = jax.random.normal(second_key, shape, jnp.float32) * (0.6 / BS ** 0.5)
    row_ids = jnp.arange(BS)[:, None]
    col_ids = jnp.arange(BS)[None, :]
    on_diag = (row_ids == col_ids).astype(jnp.float32)
    above = (col_ids > row_ids).astype(jnp.float32)
    return (diagonal * on_diag + upper * above).astype(jnp.float32)


def draw_panel_from(key, part):
    key = jax.random.fold_in(key, 7)

    def per_device(device):
        dev_key = jax.random.fold_in(key, device)
        pieces = []
        for tree_level_index in range(LEVELS):
            entries = KP * ((LEVELS - 1 - tree_level_index) * TS + TL)
            group = OWNER_DEVICES // 2 ** tree_level_index
            level_key = jax.random.fold_in(dev_key, tree_level_index)
            first_key, second_key, third_key = jax.random.split(level_key, 3)
            covering = jax.random.permutation(first_key, group).astype(jnp.int32)
            remainder = jax.random.randint(second_key, (entries - group,), 0, group).astype(jnp.int32)
            segment = jnp.concatenate([covering, remainder])
            pieces.append(jax.random.permutation(third_key, segment))
        return jnp.concatenate(pieces)
    return jax.vmap(per_device)(jnp.arange(OWNER_DEVICES)).reshape(-1).astype(jnp.int32)


def with_ends(array, stream_key, low, top_value):
    longest = array.shape.index(max(array.shape))
    spots = []
    for shift in (0, 1):
        where = [jax.random.randint(jax.random.fold_in(stream_key, axis), (), 0, length) for axis, length in enumerate(array.shape)]
        where[longest] = (where[longest] + shift) % array.shape[longest]
        spots.append(tuple(where))
    return array.at[spots[0]].set(low).at[spots[1]].set(top_value)


def levels(rng, extent, shards, smallest, top_value):
    def one(position, parts):
        draws = jax.random.uniform(jax.random.fold_in(jax.random.fold_in(rng, 6), position), (parts,), jnp.float32, smallest / len(shards), top_value / len(shards))
        return jnp.repeat(jnp.exp(draws), extent[position] // parts).reshape((-1,) + (1,) * (len(extent) - position - 1))

    gain = one(*shards[0])
    for cut in shards[1:]:
        gain = gain * one(*cut)
    return gain


def centred(stream_key, dims, width, most, cuts=(), kind=jnp.bfloat16):
    drawn = width * jax.random.normal(stream_key, dims, jnp.float32)
    if cuts:
        drawn = drawn * levels(stream_key, dims, cuts, -0.22, 0.18)
    return jnp.clip(drawn, -most, most).astype(kind)


def setup_inputs(seed: int = 0) -> dict:
    keys = jax.random.split(jax.random.key(seed), 8)
    noise_parts = centred(keys[0], (SEPARATOR_ROWS, RHS), 1.0, 6.0, ((0, 128),), jnp.float32)
    elimination_row = draw_elimination_row(jax.random.fold_in(keys[7], 71), 0)
    leaf_noise = centred(keys[2], (OWNER_DEVICES * TL * BS, RHS), 1.0, 6.0, ((0, 128),), jnp.float32)
    diag_inverse = draw_diag_inverse(jax.random.fold_in(keys[7], 71), 0)
    panels = centred(keys[4], (OWNER_DEVICES * NPAN, BS, BS), (KP * BS * LEVELS) ** -0.5, 0.125, ((0, 128),))
    panel_from = draw_panel_from(jax.random.fold_in(keys[7], 71), 0)
    send_lists = with_ends(jax.random.randint(keys[6], (OWNER_DEVICES, SENDS), 0, TS), jax.random.fold_in(keys[6], 1), 0, TS - 1).astype(jnp.int32)
    return {"noise_parts": noise_parts, "elimination_row": elimination_row, "leaf_noise": leaf_noise, "diag_inverse": diag_inverse, "panels": panels, "panel_from": panel_from, "send_lists": send_lists}


def reference(noise_parts, elimination_row, leaf_noise, diag_inverse, panels, panel_from, send_lists):
    highest = lax.Precision.HIGHEST
    ordered = jnp.zeros_like(noise_parts).at[elimination_row].set(noise_parts)
    sep_noise = ordered.reshape(OWNER_DEVICES, LEVELS, TS, BS, RHS)
    diag_tiles = diag_inverse.reshape(OWNER_DEVICES, NTILES, BS, BS)
    panel_tiles = panels.reshape(OWNER_DEVICES, NPAN, BS, BS)
    sources = panel_from.reshape(OWNER_DEVICES, NPAN)
    sep_update = jnp.zeros((OWNER_DEVICES, LEVELS, TS, BS, RHS), jnp.float32)
    leaf_update = jnp.zeros((OWNER_DEVICES, TL, BS, RHS), jnp.float32)
    sep_solved = []
    offset = 0
    send_offset = 0
    for tree_level_index in range(LEVELS):
        right_side = sep_noise[:, tree_level_index] - sep_update[:, tree_level_index]
        solution = jnp.einsum("ptij,ptjr->ptir", diag_tiles[:, tree_level_index * TS:(tree_level_index + 1) * TS], right_side, precision=highest)
        sep_solved.append(solution)
        sent_tiles = solution.astype(jnp.bfloat16)
        desc_tiles = (LEVELS - 1 - tree_level_index) * TS + TL
        entries = KP * desc_tiles
        group = OWNER_DEVICES // (2 ** tree_level_index)
        base = send_offset

        def receive(packed):
            receiving_device, panel_block, source_block = packed
            start = (receiving_device // group) * group
            senders = start + jnp.arange(group, dtype=jnp.int32)
            picks = send_lists[senders, base + receiving_device - start]
            incoming = sent_tiles[senders, picks]
            needed = incoming[source_block].astype(jnp.float32)
            products = jnp.einsum("eij,ejr->eir", panel_block.astype(jnp.float32), needed)
            return products.reshape(desc_tiles, KP, BS, RHS).sum(axis=1)

        update = lax.map(receive, (jnp.arange(OWNER_DEVICES, dtype=jnp.int32), panel_tiles[:, offset:offset + entries], sources[:, offset:offset + entries]))
        offset += entries
        send_offset += group
        sep_count = (LEVELS - 1 - tree_level_index) * TS
        sep_part = update[:, :sep_count].reshape(OWNER_DEVICES, LEVELS - 1 - tree_level_index, TS, BS, RHS)
        sep_update = sep_update.at[:, tree_level_index + 1:].add(sep_part)
        leaf_update = leaf_update + update[:, sep_count:]
    leaf_right = leaf_noise.reshape(OWNER_DEVICES, TL, BS, RHS) - leaf_update
    leaf_solved = jnp.einsum("ptij,ptjr->ptir", diag_tiles[:, LEVELS * TS:], leaf_right, precision=highest)
    sep_solution = jnp.stack(sep_solved, axis=1).reshape(SEPARATOR_ROWS, RHS)
    return sep_solution, leaf_solved.reshape(OWNER_DEVICES * TL * BS, RHS)
```

```python
import functools

import jax
import jax.numpy as jnp
from jax import lax
from jax.experimental import pallas as pl
from jax.experimental.pallas import tpu as pltpu
from jax.sharding import PartitionSpec as P

BS = 128
TS = 2
TL = 32
KP = 4
LEVELS = 4
AXES = ("leaf", "panel")
LEAF_STEP = 8
VMEM = pltpu.CompilerParams(vmem_limit_bytes=48 * 1024 * 1024)


def whole():
    return pl.BlockSpec(memory_space=pltpu.VMEM)


def split3(x):
    high = x.astype(jnp.bfloat16)
    rest = x - high.astype(jnp.float32)
    mid = rest.astype(jnp.bfloat16)
    low = (rest - mid.astype(jnp.float32)).astype(jnp.bfloat16)
    return high, mid, low


def place_rows(select, x):
    width = x.shape[1]
    parts = jnp.concatenate(split3(x), axis=1)
    out = jnp.dot(select, parts, preferred_element_type=jnp.float32)
    return out[:, :width] + out[:, width : 2 * width] + out[:, 2 * width :]


def pack_kernel(owner_ref, slot_ref, noise_ref, out_ref, places_ref):
    rows = noise_ref.shape[0]
    per_owner = 8
    owners = rows // per_owner
    owner = owner_ref[...]
    slot = slot_ref[...]
    hot = owner == lax.broadcasted_iota(jnp.int32, (owners, rows), 0)
    hot16 = hot.astype(jnp.float32).astype(jnp.bfloat16)
    before = lax.broadcasted_iota(jnp.int32, (rows, rows), 0) < lax.broadcasted_iota(
        jnp.int32, (rows, rows), 1
    )
    earlier = jnp.dot(
        hot16,
        before.astype(jnp.float32).astype(jnp.bfloat16),
        preferred_element_type=jnp.float32,
    )
    rank = jnp.sum(jnp.where(hot, earlier, 0.0), axis=0, keepdims=True)
    target = owner * per_owner + rank.astype(jnp.int32)
    select = (target == lax.broadcasted_iota(jnp.int32, (rows, rows), 0)).astype(jnp.float32)
    select = select.astype(jnp.bfloat16)
    out_ref[...] = place_rows(select, noise_ref[...])
    digit = lax.broadcasted_iota(jnp.int32, (8, rows), 0)
    digits = jnp.where(digit == 0, slot // 32, jnp.where(digit == 1, slot % 32, 0))
    moved = lax.dot_general(
        digits.astype(jnp.float32).astype(jnp.bfloat16),
        select,
        (((1,), (1,)), ((), ())),
        preferred_element_type=jnp.float32,
    )
    places_ref[...] = (moved[0:1] * 32.0 + moved[1:2]).astype(jnp.int32)


def order_rows(places_ref, arrived_ref, first, count):
    rows = arrived_ref.shape[0]
    select = places_ref[...] == first + lax.broadcasted_iota(jnp.int32, (count, rows), 0)
    return place_rows(select.astype(jnp.float32).astype(jnp.bfloat16), arrived_ref[...])


def solve(diag, right):
    return jnp.dot(
        diag, right, precision=lax.Precision.HIGHEST, preferred_element_type=jnp.float32
    )


def first_kernel(places_ref, arrived_ref, diag_ref, solved_ref, sent_ref):
    right = order_rows(places_ref, arrived_ref, 0, TS * BS)
    for t in range(TS):
        solved = solve(diag_ref[t], right[t * BS : (t + 1) * BS])
        solved_ref[t] = solved
        sent_ref[t] = solved.astype(jnp.bfloat16)


def order_kernel(places_ref, arrived_ref, out_ref):
    for tree_level in range(1, LEVELS):
        right = order_rows(places_ref, arrived_ref, tree_level * TS * BS, TS * BS)
        for t in range(TS):
            out_ref[(tree_level - 1) * TS + t] = right[t * BS : (t + 1) * BS]


def tile_update(from_ref, base, panels_ref, local, received_ref):
    left = jnp.concatenate([panels_ref[local + k] for k in range(KP)], axis=1)
    right = jnp.concatenate([received_ref[from_ref[base + k]] for k in range(KP)], axis=0)
    return jnp.dot(left, right, preferred_element_type=jnp.float32)


def level_kernel(
    offset, from_ref, received_ref, panels_ref, rights_ref, diag_ref, rest_ref, solved_ref, sent_ref
):
    tiles = rights_ref.shape[0]
    for d in range(TS):
        right = rights_ref[d] - tile_update(
            from_ref, offset + KP * d, panels_ref, KP * d, received_ref
        )
        solved = solve(diag_ref[d], right)
        solved_ref[d] = solved
        sent_ref[d] = solved.astype(jnp.bfloat16)
    for d in range(TS, tiles):
        rest_ref[d - TS] = rights_ref[d] - tile_update(
            from_ref, offset + KP * d, panels_ref, KP * d, received_ref
        )


def leaf_kernel(offset, from_ref, received_ref, panels_ref, right_ref, out_ref):
    first = offset + pl.program_id(0) * LEAF_STEP * KP
    for d in range(LEAF_STEP):
        out_ref[d] = right_ref[d] - tile_update(
            from_ref, first + KP * d, panels_ref, KP * d, received_ref
        )


def last_kernel(offset, from_ref, received_ref, panels_ref, right_ref, diag_ref, out_ref):
    first = offset + pl.program_id(0) * LEAF_STEP * KP
    for d in range(LEAF_STEP):
        right = right_ref[d] - tile_update(
            from_ref, first + KP * d, panels_ref, KP * d, received_ref
        )
        out_ref[d] = solve(diag_ref[d], right)


def entries_block(offset, count, grid):
    if grid:
        return pl.BlockSpec(
            (pl.Element(count), pl.Element(BS), pl.Element(BS)),
            lambda i, *_: (offset + i * count, 0, 0),
        )
    return pl.BlockSpec(
        (pl.Element(count), pl.Element(BS), pl.Element(BS)), lambda i, *_: (offset, 0, 0)
    )


def f32(*shape):
    return jax.ShapeDtypeStruct(shape, jnp.float32)


def b16(*shape):
    return jax.ShapeDtypeStruct(shape, jnp.bfloat16)


def per_device(
    noise_parts, elimination_row, leaf_noise, diag_inverse, panels, panel_from, send_lists
):
    owners = lax.axis_size(AXES)
    rows = noise_parts.shape[0]
    rhs = noise_parts.shape[1]
    per_owner = rows // owners
    outgoing, places = pl.pallas_call(
        pack_kernel,
        out_shape=(f32(rows, rhs), jax.ShapeDtypeStruct((1, rows), jnp.int32)),
        in_specs=[whole()] * 3,
        out_specs=(whole(), whole()),
        compiler_params=VMEM,
        name="pack",
    )(
        (elimination_row // rows).reshape(1, rows),
        (elimination_row % rows).reshape(1, rows),
        noise_parts,
    )
    arrived_at = lax.all_to_all(places.reshape(owners, per_owner), AXES, 0, 0, tiled=True)
    arrived = lax.all_to_all(outgoing.reshape(owners, per_owner, rhs), AXES, 0, 0, tiled=True)
    places = arrived_at.reshape(1, rows)
    arrived = arrived.reshape(rows, rhs)

    solved, sent = pl.pallas_call(
        first_kernel,
        grid=(1,),
        out_shape=(f32(TS, BS, rhs), b16(TS, BS, rhs)),
        in_specs=[whole(), whole(), entries_block(0, TS, False)],
        out_specs=(whole(), whole()),
        compiler_params=VMEM,
        name="first",
    )(places, arrived, diag_inverse)
    rights = pl.pallas_call(
        order_kernel,
        out_shape=f32((LEVELS - 1) * TS, BS, rhs),
        in_specs=[whole(), whole()],
        out_specs=whole(),
        compiler_params=VMEM,
        name="order",
    )(places, arrived)
    leaf_right = leaf_noise.reshape(TL, BS, rhs)
    send_row = send_lists[0]
    all_solved = [solved]
    offset = 0
    send_offset = 0
    for tree_level in range(LEVELS):
        group = owners >> tree_level
        groups = [
            list(range(g * group, (g + 1) * group)) for g in range(owners // group)
        ]
        picks = send_row[send_offset : send_offset + group]
        buffer = jnp.where((picks == 0)[:, None, None], sent[0][None], sent[1][None])
        received = lax.all_to_all(
            buffer, AXES, 0, 0, axis_index_groups=groups, tiled=True
        )
        send_offset += group
        sep_tiles = (LEVELS - 1 - tree_level) * TS
        leaf_offset = offset + KP * sep_tiles
        if tree_level < LEVELS - 1:
            first_diag = (tree_level + 1) * TS
            rest_tiles = max(sep_tiles - TS, TS)
            rest, solved, sent = pl.pallas_call(
                functools.partial(level_kernel, offset),
                grid_spec=pltpu.PrefetchScalarGridSpec(
                    num_scalar_prefetch=1,
                    grid=(1,),
                    in_specs=[
                        whole(),
                        entries_block(offset, KP * sep_tiles, False),
                        whole(),
                        entries_block(first_diag, TS, False),
                    ],
                    out_specs=(whole(), whole(), whole()),
                ),
                out_shape=(f32(rest_tiles, BS, rhs), f32(TS, BS, rhs), b16(TS, BS, rhs)),
                compiler_params=VMEM,
                name=f"level{tree_level}",
            )(panel_from, received, panels, rights, diag_inverse)
            rights = rest
            all_solved.append(solved)
        last = tree_level == LEVELS - 1
        in_specs = [
            whole(),
            entries_block(leaf_offset, KP * LEAF_STEP, True),
            entries_block(0, LEAF_STEP, True),
        ]
        operands = [panel_from, received, panels, leaf_right]
        if last:
            in_specs.append(entries_block(LEVELS * TS, LEAF_STEP, True))
            operands.append(diag_inverse)
        leaf_right = pl.pallas_call(
            functools.partial(last_kernel if last else leaf_kernel, leaf_offset),
            grid_spec=pltpu.PrefetchScalarGridSpec(
                num_scalar_prefetch=1,
                grid=(TL // LEAF_STEP,),
                in_specs=in_specs,
                out_specs=pl.BlockSpec((LEAF_STEP, BS, rhs), lambda i, *_: (i, 0, 0)),
            ),
            out_shape=f32(TL, BS, rhs),
            compiler_params=VMEM,
            name=f"leaf{tree_level}",
        )(*operands)
        offset = leaf_offset + KP * TL
    sep_solution = jnp.concatenate(all_solved, axis=0).reshape(rows, rhs)
    return (sep_solution, leaf_right.reshape(TL * BS, rhs))


def solution(mesh):
    return jax.shard_map(
        per_device,
        mesh=mesh,
        in_specs=(
            P(AXES, None),
            P(AXES),
            P(AXES, None),
            P(AXES, None, None),
            P(AXES, None, None),
            P(AXES),
            P(AXES, None),
        ),
        out_specs=(P(AXES, None), P(AXES, None)),
        check_vma=False,
    )
```

```python
import functools

import jax
import jax.numpy as jnp
from jax import lax
from jax.experimental import pallas as pl
from jax.experimental.pallas import tpu as pltpu
from jax.sharding import PartitionSpec as P

BS = 128
TS = 2
TL = 32
KP = 4
LEVELS = 4
AXES = ("leaf", "panel")
LEAF_STEP = 8
VMEM = pltpu.CompilerParams(vmem_limit_bytes=48 * 1024 * 1024)


def whole():
    return pl.BlockSpec(memory_space=pltpu.VMEM)


def halves(x):
    high = x.astype(jnp.bfloat16)
    return high, (x - high.astype(jnp.float32)).astype(jnp.bfloat16)


def hot(condition):
    return condition.astype(jnp.float32).astype(jnp.bfloat16)


def transposed_dot(a, b):
    return lax.dot_general(a, b, (((1,), (1,)), ((), ())), preferred_element_type=jnp.float32)


def pack_kernel(target_ref, noise_ref, out_ref):
    rows = noise_ref.shape[0]
    owners, per_owner, width = out_ref.shape
    target = target_ref[...]
    owner = target // rows
    slot = target % rows
    mine = owner == lax.broadcasted_iota(jnp.int32, (owners, rows), 0)
    before = lax.broadcasted_iota(jnp.int32, (rows, rows), 0) < lax.broadcasted_iota(
        jnp.int32, (rows, rows), 1
    )
    earlier = jnp.dot(hot(mine), hot(before), preferred_element_type=jnp.float32)
    rank = jnp.sum(jnp.where(mine, earlier, 0.0), axis=0, keepdims=True)
    position = owner * per_owner + rank.astype(jnp.int32)
    select = hot(position == lax.broadcasted_iota(jnp.int32, (rows, rows), 0))
    both = jnp.concatenate(halves(noise_ref[...]), axis=1)
    out = jnp.dot(select, both, preferred_element_type=jnp.float32)
    level_rows = TS * BS
    lane = lax.broadcasted_iota(jnp.int32, (BS, rows), 0)
    place = jnp.where(slot // level_rows == lane, slot % level_rows, -1)
    meta = transposed_dot(select, place.astype(jnp.float32).astype(jnp.bfloat16))
    out = jnp.concatenate([out, meta], axis=1)
    out_ref[...] = out.reshape(owners, per_owner, width).astype(jnp.bfloat16)


def order_rows(arrived_ref, tree_levels):
    owners, per_owner, width = arrived_ref.shape
    rows = owners * per_owner
    rhs = width - BS
    arrived = arrived_ref[...].astype(jnp.float32).reshape(rows, width).astype(jnp.bfloat16)
    unit = hot(
        lax.broadcasted_iota(jnp.int32, (8, BS), 0) == lax.broadcasted_iota(jnp.int32, (8, BS), 1)
    )
    places = transposed_dot(unit, arrived[:, rhs:]).astype(jnp.int32)
    out = []
    for tree_level in tree_levels:
        select = hot(
            places[tree_level : tree_level + 1]
            == lax.broadcasted_iota(jnp.int32, (TS * BS, rows), 0)
        )
        both = jnp.dot(select, arrived[:, :rhs], preferred_element_type=jnp.float32)
        out.append(both[:, : rhs // 2] + both[:, rhs // 2 :])
    return out


def solve(diag, right):
    left = jnp.concatenate(halves(diag), axis=0)
    both = jnp.concatenate(halves(right), axis=1)
    out = jnp.dot(left, both, preferred_element_type=jnp.float32)
    rows, width = diag.shape[0], right.shape[1]
    return (
        out[:rows, :width]
        + (out[:rows, width:] + out[rows:, :width])
        + out[rows:, width:]
    )


def finish(right, diag_ref, t, solved_ref, sent_ref):
    solved = solve(diag_ref[t], right)
    solved_ref[t] = solved
    sent_ref[t] = solved.astype(jnp.bfloat16)


def spread(send_offset, send_ref, sent_ref, buffer_ref):
    for j in range(buffer_ref.shape[0]):
        buffer_ref[j] = sent_ref[send_ref[send_offset + j]]


def first_kernel(send_ref, arrived_ref, diag_ref, solved_ref, buffer_ref, sent_ref):
    [right] = order_rows(arrived_ref, [0])
    for t in range(TS):
        finish(right[t * BS : (t + 1) * BS], diag_ref, t, solved_ref, sent_ref)
    spread(0, send_ref, sent_ref, buffer_ref)


def order_kernel(arrived_ref, out_ref):
    for i, right in enumerate(order_rows(arrived_ref, range(1, LEVELS))):
        for t in range(TS):
            out_ref[i * TS + t] = right[t * BS : (t + 1) * BS]


def tile_update(from_ref, base, panels_ref, local, received_ref):
    left = jnp.concatenate([panels_ref[local + k] for k in range(KP)], axis=1)
    right = jnp.concatenate([received_ref[from_ref[base + k]] for k in range(KP)], axis=0)
    return jnp.dot(left, right, preferred_element_type=jnp.float32)


def level_kernel(
    offset, send_offset, from_ref, send_ref, received_ref, panels_ref, rights_ref, diag_ref,
    rest_ref, solved_ref, buffer_ref, sent_ref,
):
    for d in range(TS):
        right = rights_ref[d] - tile_update(
            from_ref, offset + KP * d, panels_ref, KP * d, received_ref
        )
        finish(right, diag_ref, d, solved_ref, sent_ref)
    spread(send_offset, send_ref, sent_ref, buffer_ref)
    for d in range(TS, rights_ref.shape[0]):
        rest_ref[d - TS] = rights_ref[d] - tile_update(
            from_ref, offset + KP * d, panels_ref, KP * d, received_ref
        )


def leaf_kernel(offset, from_ref, received_ref, panels_ref, right_ref, out_ref):
    first = offset + pl.program_id(0) * LEAF_STEP * KP
    for d in range(LEAF_STEP):
        out_ref[d] = right_ref[d] - tile_update(
            from_ref, first + KP * d, panels_ref, KP * d, received_ref
        )


def last_kernel(offset, from_ref, received_ref, panels_ref, right_ref, diag_ref, out_ref):
    first = offset + pl.program_id(0) * LEAF_STEP * KP
    for d in range(LEAF_STEP):
        right = right_ref[d] - tile_update(
            from_ref, first + KP * d, panels_ref, KP * d, received_ref
        )
        out_ref[d] = solve(diag_ref[d], right)


def entries_block(offset, count, grid):
    if grid:
        return pl.BlockSpec(
            (pl.Element(count), pl.Element(BS), pl.Element(BS)),
            lambda i, *_: (offset + i * count, 0, 0),
        )
    return pl.BlockSpec(
        (pl.Element(count), pl.Element(BS), pl.Element(BS)), lambda i, *_: (offset, 0, 0)
    )


def f32(*shape):
    return jax.ShapeDtypeStruct(shape, jnp.float32)


def b16(*shape):
    return jax.ShapeDtypeStruct(shape, jnp.bfloat16)


def per_device(
    noise_parts, elimination_row, leaf_noise, diag_inverse, panels, panel_from, send_lists
):
    owners = lax.axis_size(AXES)
    rows = noise_parts.shape[0]
    rhs = noise_parts.shape[1]
    per_owner = rows // owners
    outgoing = pl.pallas_call(
        pack_kernel,
        out_shape=b16(owners, per_owner, 2 * rhs + BS),
        in_specs=[whole()] * 2,
        out_specs=whole(),
        compiler_params=VMEM,
        name="pack",
    )(elimination_row.reshape(1, rows), noise_parts)
    arrived = lax.all_to_all(outgoing, AXES, 0, 0, tiled=True)
    send_row = send_lists[0]
    solved, buffer = pl.pallas_call(
        first_kernel,
        grid_spec=pltpu.PrefetchScalarGridSpec(
            num_scalar_prefetch=1,
            grid=(1,),
            in_specs=[whole(), entries_block(0, TS, False)],
            out_specs=(whole(), whole()),
            scratch_shapes=[pltpu.VMEM((TS, BS, rhs), jnp.bfloat16)],
        ),
        out_shape=(f32(TS, BS, rhs), b16(owners, BS, rhs)),
        compiler_params=VMEM,
        name="first",
    )(send_row, arrived, diag_inverse)
    rights = pl.pallas_call(
        order_kernel,
        out_shape=f32((LEVELS - 1) * TS, BS, rhs),
        in_specs=[whole()],
        out_specs=whole(),
        compiler_params=VMEM,
        name="order",
    )(arrived)
    leaf_right = leaf_noise.reshape(TL, BS, rhs)
    all_solved = [solved]
    offset = 0
    send_offset = 0
    for tree_level in range(LEVELS):
        group = owners >> tree_level
        groups = [
            list(range(g * group, (g + 1) * group)) for g in range(owners // group)
        ]
        received = lax.all_to_all(
            buffer, AXES, 0, 0, axis_index_groups=groups, tiled=True
        )
        if tree_level:
            received, leaf_right = lax.optimization_barrier((received, leaf_right))
        send_offset += group
        sep_tiles = (LEVELS - 1 - tree_level) * TS
        leaf_offset = offset + KP * sep_tiles
        if tree_level < LEVELS - 1:
            first_diag = (tree_level + 1) * TS
            rest_tiles = max(sep_tiles - TS, TS)
            rights, solved, buffer = pl.pallas_call(
                functools.partial(level_kernel, offset, send_offset),
                grid_spec=pltpu.PrefetchScalarGridSpec(
                    num_scalar_prefetch=2,
                    grid=(1,),
                    in_specs=[
                        whole(),
                        entries_block(offset, KP * sep_tiles, False),
                        whole(),
                        entries_block(first_diag, TS, False),
                    ],
                    out_specs=(whole(), whole(), whole()),
                    scratch_shapes=[pltpu.VMEM((TS, BS, rhs), jnp.bfloat16)],
                ),
                out_shape=(
                    f32(rest_tiles, BS, rhs),
                    f32(TS, BS, rhs),
                    b16(group // 2, BS, rhs),
                ),
                compiler_params=VMEM,
                name=f"level{tree_level}",
            )(panel_from, send_row, received, panels, rights, diag_inverse)
            all_solved.append(solved)
        last = tree_level == LEVELS - 1
        in_specs = [
            whole(),
            entries_block(leaf_offset, KP * LEAF_STEP, True),
            entries_block(0, LEAF_STEP, True),
        ]
        operands = [panel_from, received, panels, leaf_right]
        if last:
            in_specs.append(entries_block(LEVELS * TS, LEAF_STEP, True))
            operands.append(diag_inverse)
        leaf_right = pl.pallas_call(
            functools.partial(last_kernel if last else leaf_kernel, leaf_offset),
            grid_spec=pltpu.PrefetchScalarGridSpec(
                num_scalar_prefetch=1,
                grid=(TL // LEAF_STEP,),
                in_specs=in_specs,
                out_specs=pl.BlockSpec((LEAF_STEP, BS, rhs), lambda i, *_: (i, 0, 0)),
            ),
            out_shape=f32(TL, BS, rhs),
            compiler_params=VMEM,
            name=f"leaf{tree_level}",
        )(*operands)
        offset = leaf_offset + KP * TL
    sep_solution = jnp.concatenate(all_solved, axis=0).reshape(rows, rhs)
    return (sep_solution, leaf_right.reshape(TL * BS, rhs))


def solution(mesh):
    return jax.shard_map(
        per_device,
        mesh=mesh,
        in_specs=(
            P(AXES, None),
            P(AXES),
            P(AXES, None),
            P(AXES, None, None),
            P(AXES, None, None),
            P(AXES),
            P(AXES, None),
        ),
        out_specs=(P(AXES, None), P(AXES, None)),
        check_vma=False,
    )
```

```python
import functools

import jax
import jax.numpy as jnp
from jax import lax
from jax.experimental import pallas as pl
from jax.experimental.pallas import tpu as pltpu
from jax.sharding import PartitionSpec as P

BS = 128
TS = 2
TL = 32
KP = 4
LEVELS = 4
AXES = ("leaf", "panel")
LEAF_STEP = 8
LAST_STEP = 4
PIECES = 4
VMEM = pltpu.CompilerParams(vmem_limit_bytes=20 * 1024 * 1024)


def whole():
    return pl.BlockSpec(memory_space=pltpu.VMEM)


def halves(x):
    high = x.astype(jnp.bfloat16)
    return high, (x - high.astype(jnp.float32)).astype(jnp.bfloat16)


def hot(condition):
    return condition.astype(jnp.float32).astype(jnp.bfloat16)


def transposed_dot(a, b):
    return lax.dot_general(a, b, (((1,), (1,)), ((), ())), preferred_element_type=jnp.float32)


def pack_kernel(target_ref, noise_ref, out_ref):
    rows = noise_ref.shape[0]
    owners, per_owner, width = out_ref.shape
    target = target_ref[...]
    owner = target // rows
    slot = target % rows
    mine = owner == lax.broadcasted_iota(jnp.int32, (owners, rows), 0)
    before = lax.broadcasted_iota(jnp.int32, (rows, rows), 0) < lax.broadcasted_iota(
        jnp.int32, (rows, rows), 1
    )
    earlier = jnp.dot(hot(mine), hot(before), preferred_element_type=jnp.float32)
    rank = jnp.sum(jnp.where(mine, earlier, 0.0), axis=0, keepdims=True)
    position = owner * per_owner + rank.astype(jnp.int32)
    select = hot(position == lax.broadcasted_iota(jnp.int32, (rows, rows), 0))
    both = jnp.concatenate(halves(noise_ref[...]), axis=1)
    out = jnp.dot(select, both, preferred_element_type=jnp.float32)
    level_rows = TS * BS
    lane = lax.broadcasted_iota(jnp.int32, (BS, rows), 0)
    place = jnp.where(slot // level_rows == lane, slot % level_rows, -1)
    meta = transposed_dot(select, place.astype(jnp.float32).astype(jnp.bfloat16))
    out = jnp.concatenate([out, meta], axis=1)
    out_ref[...] = out.reshape(owners, per_owner, width).astype(jnp.bfloat16)


def order_rows(arrived_ref, tree_levels):
    owners, per_owner, width = arrived_ref.shape
    rows = owners * per_owner
    rhs = width - BS
    arrived = arrived_ref[...].astype(jnp.float32).reshape(rows, width).astype(jnp.bfloat16)
    unit = hot(
        lax.broadcasted_iota(jnp.int32, (8, BS), 0) == lax.broadcasted_iota(jnp.int32, (8, BS), 1)
    )
    places = transposed_dot(unit, arrived[:, rhs:]).astype(jnp.int32)
    out = []
    for tree_level in tree_levels:
        select = hot(
            places[tree_level : tree_level + 1]
            == lax.broadcasted_iota(jnp.int32, (TS * BS, rows), 0)
        )
        both = jnp.dot(select, arrived[:, :rhs], preferred_element_type=jnp.float32)
        out.append(both[:, : rhs // 2] + both[:, rhs // 2 :])
    return out


def solve(diag, right):
    left = jnp.concatenate(halves(diag), axis=0)
    both = jnp.concatenate(halves(right), axis=1)
    out = jnp.dot(left, both, preferred_element_type=jnp.float32)
    rows, width = diag.shape[0], right.shape[1]
    return (
        out[:rows, :width]
        + (out[:rows, width:] + out[rows:, :width])
        + out[rows:, width:]
    )


def finish(right, diag_ref, t, solved_ref, sent_ref):
    solved = solve(diag_ref[t], right)
    solved_ref[t] = solved
    sent_ref[t] = solved.astype(jnp.bfloat16)


def spread(send_offset, send_ref, sent_ref, made_ref, buffer_ref, done):
    count = made_ref.shape[0] // PIECES
    copies = []
    for piece in range(PIECES):
        for j in range(piece * count, (piece + 1) * count):
            made_ref[j] = sent_ref[send_ref[send_offset + j]]
        part = pl.ds(piece * count, count)
        copies.append(pltpu.make_async_copy(made_ref.at[part], buffer_ref.at[part], done.at[piece]))
        copies[-1].start()
    return copies


def first_kernel(send_ref, arrived_ref, diag_ref, solved_ref, buffer_ref, sent_ref, made_ref, done):
    [right] = order_rows(arrived_ref, [0])
    for t in range(TS):
        finish(right[t * BS : (t + 1) * BS], diag_ref, t, solved_ref, sent_ref)
    for copy in spread(0, send_ref, sent_ref, made_ref, buffer_ref, done):
        copy.wait()


def order_kernel(arrived_ref, out_ref):
    for i, right in enumerate(order_rows(arrived_ref, range(1, LEVELS))):
        for t in range(TS):
            out_ref[i * TS + t] = right[t * BS : (t + 1) * BS]


def tile_update(panels_ref, local, tile):
    left = jnp.concatenate([panels_ref[local + k] for k in range(KP)], axis=1)
    right = jnp.concatenate([tile(k) for k in range(KP)], axis=0)
    return jnp.dot(left, right, preferred_element_type=jnp.float32)


def level_kernel(
    offset, send_offset, from_ref, send_ref, received_ref, panels_ref, rights_ref, diag_ref,
    rest_ref, solved_ref, buffer_ref, near_ref, sent_ref, made_ref, arrived, done,
):
    tiles = rights_ref.shape[0]
    fetches = []
    for e in range(tiles * KP):
        fetches.append(
            pltpu.make_async_copy(
                received_ref.at[from_ref[offset + e]], near_ref.at[e], arrived.at[e]
            )
        )
        fetches[-1].start()

    def right_side(d):
        for k in range(KP):
            fetches[KP * d + k].wait()
        return rights_ref[d] - tile_update(panels_ref, KP * d, lambda k: near_ref[KP * d + k])

    for d in range(TS):
        finish(right_side(d), diag_ref, d, solved_ref, sent_ref)
    copies = spread(send_offset, send_ref, sent_ref, made_ref, buffer_ref, done)
    for d in range(TS, tiles):
        rest_ref[d - TS] = right_side(d)
    for copy in copies:
        copy.wait()


def leaf_update(offset, from_ref, received_ref, panels_ref, right_ref):
    count = right_ref.shape[0]
    first = offset + pl.program_id(0) * count * KP
    for d in range(count):
        yield right_ref[d] - tile_update(
            panels_ref, KP * d, lambda k: received_ref[from_ref[first + KP * d + k]]
        )


def leaf_kernel(offset, from_ref, received_ref, panels_ref, right_ref, out_ref):
    for d, right in enumerate(leaf_update(offset, from_ref, received_ref, panels_ref, right_ref)):
        out_ref[d] = right


def last_kernel(offset, from_ref, received_ref, panels_ref, right_ref, diag_ref, out_ref):
    rights = list(leaf_update(offset, from_ref, received_ref, panels_ref, right_ref))
    for d, right in enumerate(rights):
        out_ref[d] = solve(diag_ref[d], right)


def entries_block(offset, count):
    return pl.BlockSpec(
        (pl.Element(count), pl.Element(BS), pl.Element(BS)),
        lambda i, *_: (offset + i * count, 0, 0),
    )


def streamed(x):
    return pltpu.with_memory_space_constraint(x, pltpu.HBM)


def f32(*shape):
    return jax.ShapeDtypeStruct(shape, jnp.float32)


def b16(*shape):
    return jax.ShapeDtypeStruct(shape, jnp.bfloat16)


def per_device(
    noise_parts, elimination_row, leaf_noise, diag_inverse, panels, panel_from, send_lists
):
    owners = lax.axis_size(AXES)
    rows = noise_parts.shape[0]
    rhs = noise_parts.shape[1]
    per_owner = rows // owners
    outgoing = pl.pallas_call(
        pack_kernel,
        out_shape=b16(owners, per_owner, 2 * rhs + BS),
        in_specs=[whole()] * 2,
        out_specs=whole(),
        compiler_params=VMEM,
        name="pack",
    )(elimination_row.reshape(1, rows), noise_parts)
    arrived = lax.all_to_all(outgoing, AXES, 0, 0, tiled=True)
    send_row = send_lists[0]
    stream = streamed(panels)
    solved, buffer = pl.pallas_call(
        first_kernel,
        grid_spec=pltpu.PrefetchScalarGridSpec(
            num_scalar_prefetch=1,
            grid=(1,),
            in_specs=[whole(), whole()],
            out_specs=(entries_block(0, TS), pl.BlockSpec(memory_space=pltpu.HBM)),
            scratch_shapes=[
                pltpu.VMEM((TS, BS, rhs), jnp.bfloat16),
                pltpu.VMEM((owners, BS, rhs), jnp.bfloat16),
                pltpu.SemaphoreType.DMA((PIECES,)),
            ],
        ),
        out_shape=(
            pltpu.HBM((TS, BS, rhs), jnp.float32),
            pltpu.HBM((owners, BS, rhs), jnp.bfloat16),
        ),
        compiler_params=VMEM,
        name="first",
    )(send_row, arrived, diag_inverse[:TS])
    rights = pl.pallas_call(
        order_kernel,
        out_shape=f32((LEVELS - 1) * TS, BS, rhs),
        in_specs=[whole()],
        out_specs=whole(),
        compiler_params=VMEM,
        name="order",
    )(arrived)
    leaf_right = leaf_noise.reshape(TL, BS, rhs)
    all_solved = [solved]
    offset = 0
    send_offset = 0
    for tree_level in range(LEVELS):
        group = owners >> tree_level
        groups = [
            list(range(g * group, (g + 1) * group)) for g in range(owners // group)
        ]
        received = lax.all_to_all(
            buffer, AXES, 0, 0, axis_index_groups=groups, tiled=True
        )
        if tree_level:
            received, leaf_right = lax.optimization_barrier((received, leaf_right))
        send_offset += group
        sep_tiles = (LEVELS - 1 - tree_level) * TS
        leaf_offset = offset + KP * sep_tiles
        if tree_level < LEVELS - 1:
            first_diag = (tree_level + 1) * TS
            level_diag = diag_inverse[first_diag : first_diag + TS]
            rest_tiles = max(sep_tiles - TS, TS)
            rights, solved, buffer = pl.pallas_call(
                functools.partial(level_kernel, offset, send_offset),
                grid_spec=pltpu.PrefetchScalarGridSpec(
                    num_scalar_prefetch=2,
                    grid=(1,),
                    in_specs=[
                        pl.BlockSpec(memory_space=pl.ANY),
                        whole(),
                        whole(),
                        whole(),
                    ],
                    out_specs=(
                        whole(),
                        entries_block(0, TS),
                        pl.BlockSpec(memory_space=pltpu.HBM),
                    ),
                    scratch_shapes=[
                        pltpu.VMEM((KP * sep_tiles, BS, rhs), jnp.bfloat16),
                        pltpu.VMEM((TS, BS, rhs), jnp.bfloat16),
                        pltpu.VMEM((group // 2, BS, rhs), jnp.bfloat16),
                        pltpu.SemaphoreType.DMA((KP * sep_tiles,)),
                        pltpu.SemaphoreType.DMA((PIECES,)),
                    ],
                ),
                out_shape=(
                    f32(rest_tiles, BS, rhs),
                    pltpu.HBM((TS, BS, rhs), jnp.float32),
                    pltpu.HBM((group // 2, BS, rhs), jnp.bfloat16),
                ),
                compiler_params=VMEM,
                name=f"level{tree_level}",
            )(panel_from, send_row, received, panels[offset : offset + KP * sep_tiles], rights, level_diag)
            all_solved.append(solved)
        last = tree_level == LEVELS - 1
        step = LAST_STEP if last else LEAF_STEP
        in_specs = [
            whole(),
            entries_block(leaf_offset, KP * step),
            entries_block(0, step),
        ]
        operands = [panel_from, received, stream, streamed(leaf_right)]
        if last:
            in_specs.append(entries_block(LEVELS * TS, step))
            operands.append(streamed(diag_inverse))
        leaf_right = pl.pallas_call(
            functools.partial(last_kernel if last else leaf_kernel, leaf_offset),
            grid_spec=pltpu.PrefetchScalarGridSpec(
                num_scalar_prefetch=1,
                grid=(TL // step,),
                in_specs=in_specs,
                out_specs=pl.BlockSpec((step, BS, rhs), lambda i, *_: (i, 0, 0)),
            ),
            out_shape=pltpu.HBM((TL, BS, rhs), jnp.float32),
            compiler_params=VMEM,
            name=f"leaf{tree_level}",
        )(*operands)
        offset = leaf_offset + KP * TL
    sep_solution = jnp.concatenate(all_solved, axis=0).reshape(rows, rhs)
    return (sep_solution, leaf_right.reshape(TL * BS, rhs))


def solution(mesh):
    return jax.shard_map(
        per_device,
        mesh=mesh,
        in_specs=(
            P(AXES, None),
            P(AXES),
            P(AXES, None),
            P(AXES, None, None),
            P(AXES, None, None),
            P(AXES),
            P(AXES, None),
        ),
        out_specs=(P(AXES, None), P(AXES, None)),
        check_vma=False,
    )
```

```python
import functools

import jax
import jax.numpy as jnp
from jax import lax
from jax.experimental import pallas as pl
from jax.experimental.pallas import tpu as pltpu
from jax.sharding import PartitionSpec as P

BS = 128
TS = 2
TL = 32
KP = 4
LEVELS = 4
AXES = ("leaf", "panel")
LEAF_STEP = 8
LAST_STEP = 8
PIECES = 4
VMEM = pltpu.CompilerParams(vmem_limit_bytes=16 * 1024 * 1024)


def in_hbm():
    return pl.BlockSpec(memory_space=pltpu.HBM)


def whole():
    return pl.BlockSpec(memory_space=pltpu.VMEM)


def halves(x):
    high = x.astype(jnp.bfloat16)
    return high, (x - high.astype(jnp.float32)).astype(jnp.bfloat16)


def hot(condition):
    return condition.astype(jnp.float32).astype(jnp.bfloat16)


def transposed_dot(a, b):
    return lax.dot_general(a, b, (((1,), (1,)), ((), ())), preferred_element_type=jnp.float32)


def pack_kernel(target_ref, noise_ref, out_ref):
    rows = noise_ref.shape[0]
    owners, per_owner, width = out_ref.shape
    target = target_ref[...]
    owner = target // rows
    slot = target % rows
    mine = owner == lax.broadcasted_iota(jnp.int32, (owners, rows), 0)
    before = lax.broadcasted_iota(jnp.int32, (rows, rows), 0) < lax.broadcasted_iota(
        jnp.int32, (rows, rows), 1
    )
    earlier = jnp.dot(hot(mine), hot(before), preferred_element_type=jnp.float32)
    rank = jnp.sum(jnp.where(mine, earlier, 0.0), axis=0, keepdims=True)
    position = owner * per_owner + rank.astype(jnp.int32)
    select = hot(position == lax.broadcasted_iota(jnp.int32, (rows, rows), 0))
    both = jnp.concatenate(halves(noise_ref[...]), axis=1)
    out = jnp.dot(select, both, preferred_element_type=jnp.float32)
    level_rows = TS * BS
    lane = lax.broadcasted_iota(jnp.int32, (BS, rows), 0)
    place = jnp.where(slot // level_rows == lane, slot % level_rows, -1)
    meta = transposed_dot(select, place.astype(jnp.float32).astype(jnp.bfloat16))
    out = jnp.concatenate([out, meta], axis=1)
    out_ref[...] = out.reshape(owners, per_owner, width).astype(jnp.bfloat16)


def order_rows(arrived_ref, tree_levels):
    owners, per_owner, width = arrived_ref.shape
    rows = owners * per_owner
    rhs = width - BS
    arrived = arrived_ref[...].astype(jnp.float32).reshape(rows, width).astype(jnp.bfloat16)
    unit = hot(
        lax.broadcasted_iota(jnp.int32, (8, BS), 0) == lax.broadcasted_iota(jnp.int32, (8, BS), 1)
    )
    places = transposed_dot(unit, arrived[:, rhs:]).astype(jnp.int32)
    out = []
    for tree_level in tree_levels:
        select = hot(
            places[tree_level : tree_level + 1]
            == lax.broadcasted_iota(jnp.int32, (TS * BS, rows), 0)
        )
        both = jnp.dot(select, arrived[:, :rhs], preferred_element_type=jnp.float32)
        out.append(both[:, : rhs // 2] + both[:, rhs // 2 :])
    return out


def solve(diag, right):
    left = jnp.concatenate(halves(diag), axis=0)
    both = jnp.concatenate(halves(right), axis=1)
    out = jnp.dot(left, both, preferred_element_type=jnp.float32)
    rows, width = diag.shape[0], right.shape[1]
    return (
        out[:rows, :width]
        + (out[:rows, width:] + out[rows:, :width])
        + out[rows:, width:]
    )


def finish(right, diag_ref, t, solved_ref, sent_ref):
    solved = solve(diag_ref[t], right)
    solved_ref[t] = solved
    sent_ref[t] = solved.astype(jnp.bfloat16)


def first_kernel(arrived_ref, diag_hbm, solved_ref, sent_ref, diag_ref, arrived):
    fetch = pltpu.make_async_copy(diag_hbm.at[pl.ds(0, TS)], diag_ref, arrived)
    fetch.start()
    [right] = order_rows(arrived_ref, [0])
    fetch.wait()
    for t in range(TS):
        finish(right[t * BS : (t + 1) * BS], diag_ref, t, solved_ref, sent_ref)


def order_kernel(arrived_ref, out_ref):
    for i, right in enumerate(order_rows(arrived_ref, range(1, LEVELS))):
        for t in range(TS):
            out_ref[i * TS + t] = right[t * BS : (t + 1) * BS]


def tile_update(panels_ref, local, tile):
    left = jnp.concatenate([panels_ref[local + k] for k in range(KP)], axis=1)
    right = jnp.concatenate([tile(k) for k in range(KP)], axis=0)
    return jnp.dot(left, right, preferred_element_type=jnp.float32)


def start(*pairs):
    copies = [pltpu.make_async_copy(*pair) for pair in pairs]
    for copy in copies:
        copy.start()
    return copies


def level_kernel(
    offset, first_diag, from_hbm, received_ref, panels_hbm, rights_hbm, diag_hbm,
    rest_ref, solved_ref, sent_ref,
    from_ref, panels_ref, rights_ref, diag_ref, arrived, near_ref=None, near_arrived=None,
):
    tiles = rights_ref.shape[0]
    copies = start(
        (from_hbm, from_ref, arrived.at[0]),
        (panels_hbm.at[pl.ds(offset, KP * tiles)], panels_ref, arrived.at[1]),
        (rights_hbm, rights_ref, arrived.at[2]),
        (diag_hbm.at[pl.ds(first_diag, TS)], diag_ref, arrived.at[3]),
    )
    if near_ref is not None:
        count = received_ref.shape[0] // PIECES
        for piece in range(PIECES):
            part = pl.ds(piece * count, count)
            copies += start((received_ref.at[part], near_ref.at[part], near_arrived.at[piece]))
        received_ref = near_ref
    for copy in copies:
        copy.wait()
    for d in range(tiles):
        right = rights_ref[d] - tile_update(
            panels_ref, KP * d, lambda k: received_ref[from_ref[offset + KP * d + k]]
        )
        if d < TS:
            finish(right, diag_ref, d, solved_ref, sent_ref)
        else:
            rest_ref[d - TS] = right


def leaf_kernel(offset, from_ref, received_ref, panels_ref, right_ref, out_ref):
    first = offset + pl.program_id(0) * LEAF_STEP * KP
    for d in range(LEAF_STEP):
        out_ref[d] = right_ref[d] - tile_update(
            panels_ref, KP * d, lambda k: received_ref[from_ref[first + KP * d + k]]
        )


def last_kernel(
    offset, from_hbm, received_ref, panels_hbm, right_hbm, diag_hbm, out_hbm,
    from_ref, panels_ref, right_ref, diag_ref, out_ref, arrived, left,
):
    parts = TL // LAST_STEP
    [chosen] = start((from_hbm, from_ref, arrived.at[3 * parts]))
    loads = []
    for part in range(parts):
        first = part * LAST_STEP
        tiles = pl.ds(first, LAST_STEP)
        entries = pl.ds(KP * first, KP * LAST_STEP)
        loads.append(
            start(
                (
                    panels_hbm.at[pl.ds(offset + KP * first, KP * LAST_STEP)],
                    panels_ref.at[entries],
                    arrived.at[3 * part],
                ),
                (right_hbm.at[tiles], right_ref.at[tiles], arrived.at[3 * part + 1]),
                (
                    diag_hbm.at[pl.ds(LEVELS * TS + first, LAST_STEP)],
                    diag_ref.at[tiles],
                    arrived.at[3 * part + 2],
                ),
            )
        )
    chosen.wait()
    stores = []
    for part in range(parts):
        for copy in loads[part]:
            copy.wait()
        tiles = range(part * LAST_STEP, (part + 1) * LAST_STEP)
        rights = [
            right_ref[t]
            - tile_update(
                panels_ref, KP * t, lambda k: received_ref[from_ref[offset + KP * t + k]]
            )
            for t in tiles
        ]
        for t, right in zip(tiles, rights):
            out_ref[t] = solve(diag_ref[t], right)
        done = pl.ds(part * LAST_STEP, LAST_STEP)
        stores += start((out_ref.at[done], out_hbm.at[done], left.at[part]))
    for copy in stores:
        copy.wait()


def entries_block(offset, count):
    return pl.BlockSpec(
        (pl.Element(count), pl.Element(BS), pl.Element(BS)),
        lambda i, *_: (offset + i * count, 0, 0),
    )


def streamed(x):
    return pltpu.with_memory_space_constraint(x, pltpu.HBM)


def f32(*shape):
    return jax.ShapeDtypeStruct(shape, jnp.float32)


def b16(*shape):
    return jax.ShapeDtypeStruct(shape, jnp.bfloat16)


def per_device(
    noise_parts, elimination_row, leaf_noise, diag_inverse, panels, panel_from, send_lists
):
    owners = lax.axis_size(AXES)
    rows = noise_parts.shape[0]
    rhs = noise_parts.shape[1]
    per_owner = rows // owners
    outgoing = pl.pallas_call(
        pack_kernel,
        out_shape=b16(owners, per_owner, 2 * rhs + BS),
        in_specs=[whole()] * 2,
        out_specs=whole(),
        compiler_params=VMEM,
        name="pack",
    )(elimination_row.reshape(1, rows), noise_parts)
    arrived = lax.all_to_all(outgoing, AXES, 0, 0, tiled=True)
    send_row = send_lists[0]
    stream = streamed(panels)
    diag_stream = streamed(diag_inverse)
    from_stream = streamed(panel_from)
    solved, sent = pl.pallas_call(
        first_kernel,
        out_shape=(f32(TS, BS, rhs), b16(TS, BS, rhs)),
        in_specs=[whole(), in_hbm()],
        out_specs=(whole(), whole()),
        scratch_shapes=[pltpu.VMEM((TS, BS, BS), jnp.float32), pltpu.SemaphoreType.DMA],
        compiler_params=VMEM,
        name="first",
    )(arrived, diag_stream)
    rights = pl.pallas_call(
        order_kernel,
        out_shape=f32((LEVELS - 1) * TS, BS, rhs),
        in_specs=[whole()],
        out_specs=whole(),
        compiler_params=VMEM,
        name="order",
    )(arrived)
    leaf_right = leaf_noise.reshape(TL, BS, rhs)
    all_solved = [solved]
    offset = 0
    send_offset = 0
    for tree_level in range(LEVELS):
        group = owners >> tree_level
        groups = [
            list(range(g * group, (g + 1) * group)) for g in range(owners // group)
        ]
        picks = send_row[send_offset : send_offset + group]
        buffer = jnp.where((picks == 0)[:, None, None], sent[0][None], sent[1][None])
        received = lax.all_to_all(
            buffer, AXES, 0, 0, axis_index_groups=groups, tiled=True
        )
        if tree_level:
            received, leaf_right = lax.optimization_barrier((received, leaf_right))
        send_offset += group
        sep_tiles = (LEVELS - 1 - tree_level) * TS
        leaf_offset = offset + KP * sep_tiles
        if tree_level < LEVELS - 1:
            first_diag = (tree_level + 1) * TS
            rest_tiles = max(sep_tiles - TS, TS)
            fetch = tree_level == 0
            scratch = [
                pltpu.SMEM(panel_from.shape, jnp.int32),
                pltpu.VMEM((KP * sep_tiles, BS, BS), jnp.bfloat16),
                pltpu.VMEM((sep_tiles, BS, rhs), jnp.float32),
                pltpu.VMEM((TS, BS, BS), jnp.float32),
                pltpu.SemaphoreType.DMA((4,)),
            ]
            if fetch:
                scratch += [
                    pltpu.VMEM((group, BS, rhs), jnp.bfloat16),
                    pltpu.SemaphoreType.DMA((PIECES,)),
                ]
            rights, solved, sent = pl.pallas_call(
                functools.partial(level_kernel, offset, first_diag),
                in_specs=[in_hbm(), in_hbm() if fetch else whole()] + [in_hbm()] * 3,
                out_specs=(whole(),) * 3,
                out_shape=(f32(rest_tiles, BS, rhs), f32(TS, BS, rhs), b16(TS, BS, rhs)),
                scratch_shapes=scratch,
                compiler_params=VMEM,
                name=f"level{tree_level}",
            )(
                from_stream,
                streamed(received) if fetch else received,
                stream,
                streamed(rights),
                diag_stream,
            )
            all_solved.append(solved)
            leaf_right = pl.pallas_call(
                functools.partial(leaf_kernel, leaf_offset),
                grid_spec=pltpu.PrefetchScalarGridSpec(
                    num_scalar_prefetch=1,
                    grid=(TL // LEAF_STEP,),
                    in_specs=[
                        whole(),
                        entries_block(leaf_offset, KP * LEAF_STEP),
                        entries_block(0, LEAF_STEP),
                    ],
                    out_specs=entries_block(0, LEAF_STEP),
                ),
                out_shape=pltpu.HBM((TL, BS, rhs), jnp.float32),
                compiler_params=VMEM,
                name=f"leaf{tree_level}",
            )(panel_from, received, stream, streamed(leaf_right))
        else:
            parts = TL // LAST_STEP
            leaf_right = pl.pallas_call(
                functools.partial(last_kernel, leaf_offset),
                in_specs=[in_hbm(), whole()] + [in_hbm()] * 3,
                out_specs=in_hbm(),
                out_shape=pltpu.HBM((TL, BS, rhs), jnp.float32),
                scratch_shapes=[
                    pltpu.SMEM(panel_from.shape, jnp.int32),
                    pltpu.VMEM((KP * TL, BS, BS), jnp.bfloat16),
                    pltpu.VMEM((TL, BS, rhs), jnp.float32),
                    pltpu.VMEM((TL, BS, BS), jnp.float32),
                    pltpu.VMEM((TL, BS, rhs), jnp.float32),
                    pltpu.SemaphoreType.DMA((3 * parts + 1,)),
                    pltpu.SemaphoreType.DMA((parts,)),
                ],
                compiler_params=VMEM,
                name="last",
            )(from_stream, received, stream, streamed(leaf_right), diag_stream)
        offset = leaf_offset + KP * TL
    sep_solution = jnp.concatenate(all_solved, axis=0).reshape(rows, rhs)
    return (sep_solution, leaf_right.reshape(TL * BS, rhs))


def solution(mesh):
    return jax.shard_map(
        per_device,
        mesh=mesh,
        in_specs=(
            P(AXES, None),
            P(AXES),
            P(AXES, None),
            P(AXES, None, None),
            P(AXES, None, None),
            P(AXES),
            P(AXES, None),
        ),
        out_specs=(P(AXES, None), P(AXES, None)),
        check_vma=False,
    )
```

```python
import functools

import jax
import jax.numpy as jnp
from jax import lax
from jax.experimental import pallas as pl
from jax.experimental.pallas import tpu as pltpu
from jax.sharding import PartitionSpec as P

BS = 128
TS = 2
TL = 32
KP = 4
LEVELS = 4
AXES = ("leaf", "panel")
LEAF_STEP = 8
LAST_STEP = 8
SIDE = 4
CUTS = (0, 48, 96, 128)
ORDERS = ("xzy", "zyx", "yxz")
VMEM = pltpu.CompilerParams(vmem_limit_bytes=16 * 1024 * 1024)


def in_hbm():
    return pl.BlockSpec(memory_space=pltpu.HBM)


def whole():
    return pl.BlockSpec(memory_space=pltpu.VMEM)


def halves(x):
    high = x.astype(jnp.bfloat16)
    return high, (x - high.astype(jnp.float32)).astype(jnp.bfloat16)


def hot(condition):
    return condition.astype(jnp.float32).astype(jnp.bfloat16)


def transposed_dot(a, b):
    return lax.dot_general(a, b, (((1,), (1,)), ((), ())), preferred_element_type=jnp.float32)


def pack_kernel(target_ref, send_ref, noise_ref, out_ref):
    rows = noise_ref.shape[0]
    owners, per_owner, width = out_ref.shape
    target = target_ref[...]
    owner = target // rows
    slot = target % rows
    mine = owner == lax.broadcasted_iota(jnp.int32, (owners, rows), 0)
    before = lax.broadcasted_iota(jnp.int32, (rows, rows), 0) < lax.broadcasted_iota(
        jnp.int32, (rows, rows), 1
    )
    earlier = jnp.dot(hot(mine), hot(before), preferred_element_type=jnp.float32)
    rank = jnp.sum(jnp.where(mine, earlier, 0.0), axis=0, keepdims=True)
    position = owner * per_owner + rank.astype(jnp.int32)
    select = hot(position == lax.broadcasted_iota(jnp.int32, (rows, rows), 0))
    both = jnp.concatenate(halves(noise_ref[...]), axis=1)
    out = jnp.dot(select, both, preferred_element_type=jnp.float32)
    level_rows = TS * BS
    lane = lax.broadcasted_iota(jnp.int32, (BS, rows), 0)
    place = jnp.where(slot // level_rows == lane, slot % level_rows, -1)
    row = lax.broadcasted_iota(jnp.int32, (BS, owners), 0)
    picks = send_ref[:, :owners]
    theirs = (owner ^ SIDE) == lax.broadcasted_iota(jnp.int32, (owners, rows), 0)
    picked = jnp.dot(
        hot((picks > 0) & (row == LEVELS)), hot(mine), preferred_element_type=jnp.float32
    ) + jnp.dot(
        hot((picks > 0) & (row == LEVELS + 1)), hot(theirs), preferred_element_type=jnp.float32
    )
    place = jnp.where(lane < LEVELS, place.astype(jnp.float32), picked)
    meta = transposed_dot(select, place.astype(jnp.bfloat16))
    out = jnp.concatenate([out, meta], axis=1)
    out_ref[...] = out.reshape(owners, per_owner, width).astype(jnp.bfloat16)


def arrived_parts(arrived_ref):
    owners, per_owner, width = arrived_ref.shape
    rows = owners * per_owner
    arrived = arrived_ref[...].astype(jnp.float32).reshape(rows, width).astype(jnp.bfloat16)
    unit = hot(
        lax.broadcasted_iota(jnp.int32, (8, BS), 0) == lax.broadcasted_iota(jnp.int32, (8, BS), 1)
    )
    places = transposed_dot(unit, arrived[:, width - BS :]).astype(jnp.int32)
    return arrived[:, : width - BS], places


def order_rows(arrived, places, tree_level):
    rows, width = arrived.shape
    select = hot(
        places[tree_level : tree_level + 1]
        == lax.broadcasted_iota(jnp.int32, (TS * BS, rows), 0)
    )
    both = jnp.dot(select, arrived, preferred_element_type=jnp.float32)
    return both[:, : width // 2] + both[:, width // 2 :]


def solve(diag, right):
    left = jnp.concatenate(halves(diag), axis=0)
    both = jnp.concatenate(halves(right), axis=1)
    out = jnp.dot(left, both, preferred_element_type=jnp.float32)
    rows, width = diag.shape[0], right.shape[1]
    return (
        out[:rows, :width]
        + (out[:rows, width:] + out[rows:, :width])
        + out[rows:, width:]
    )


def finish(right, diag_ref, t, solved_ref, sent_ref):
    solved = solve(diag_ref[t], right)
    solved_ref[t] = solved
    sent_ref[t] = solved.astype(jnp.bfloat16)


def first_kernel(arrived_ref, diag_hbm, solved_ref, sent_ref, diag_ref, arrived):
    fetch = pltpu.make_async_copy(diag_hbm.at[pl.ds(0, TS)], diag_ref, arrived)
    fetch.start()
    right = order_rows(*arrived_parts(arrived_ref), 0)
    fetch.wait()
    for t in range(TS):
        finish(right[t * BS : (t + 1) * BS], diag_ref, t, solved_ref, sent_ref)


def order_kernel(arrived_ref, out_ref, picks_ref):
    arrived, places = arrived_parts(arrived_ref)
    for i in range(LEVELS - 1):
        right = order_rows(arrived, places, i + 1)
        for t in range(TS):
            out_ref[i * TS + t] = right[t * BS : (t + 1) * BS]
    picks_ref[...] = places[LEVELS : LEVELS + 2]


def step_pairs(axis, second):
    pairs = []
    for device in range(2 * SIDE**3):
        at = {
            "x": device % SIDE,
            "c": device // SIDE % 2,
            "z": device // (2 * SIDE) % SIDE,
            "y": device // (2 * SIDE * SIDE),
        }
        up = (at[axis] + at["c"] + second) % 2 == 0
        at[axis] = (at[axis] + (1 if up else -1)) % SIDE
        pairs.append((device, ((at["y"] * SIDE + at["z"]) * 2 + at["c"]) * SIDE + at["x"]))
    return pairs


def gather_core(sent):
    parts = [sent[:, a:b] for a, b in zip(CUTS, CUTS[1:])]
    for step in range(2 * len(ORDERS[0])):
        arriving = [
            lax.ppermute(part, AXES, step_pairs(order[step // 2], step % 2))
            for part, order in zip(parts, ORDERS)
        ]
        parts = [jnp.concatenate(both, axis=0) for both in zip(parts, arriving)]
    return parts


def swap_core(x):
    return lax.ppermute(x, AXES, [(i, i ^ SIDE) for i in range(2 * SIDE**3)])


def same_core(position, at_ref):
    return (position // SIDE) % 2 == at_ref[3]


def take(parts, at_ref, position, pick):
    core = at_ref[3]

    def place(axis, there):
        here = at_ref["xyz".index(axis)]
        away = there - here
        away = jnp.where((here + core) % 2 == 0, away, -away) & (SIDE - 1)
        return away ^ (away >> 1)

    there = {
        "x": position % SIDE,
        "z": position // (2 * SIDE) % SIDE,
        "y": position // (2 * SIDE * SIDE),
    }
    spots = {axis: place(axis, there[axis]) for axis in there}
    for part, order in zip(parts, ORDERS):
        at = 0
        for axis in reversed(order):
            at = at * SIDE + spots[axis]
        yield part[at * TS + pick]


def near_kernel(at_ref, picks_ref, mine_ref, theirs_ref, a_ref, b_ref, c_ref, own_ref, other_ref):
    for which, (from_ref, out_ref) in enumerate(((mine_ref, own_ref), (theirs_ref, other_ref))):
        for e in range(out_ref.shape[0]):
            position = from_ref[e]
            blocks = take((a_ref, b_ref, c_ref), at_ref, position, picks_ref[which, position * 8])
            for first, block in zip(CUTS, blocks):
                out_ref[e, first : first + block.shape[0]] = block


def spread_kernel(at_ref, picks_ref, a_ref, b_ref, c_ref, own_ref, other_ref):
    def body(i, carry):
        position = i // SIDE * (2 * SIDE) + at_ref[3] * SIDE + i % SIDE
        for which, out_ref in enumerate((own_ref, other_ref)):
            blocks = take((a_ref, b_ref, c_ref), at_ref, position, picks_ref[which, position * 8])
            for first, block in zip(CUTS, blocks):
                out_ref[i, first : first + block.shape[0]] = block
        return carry

    lax.fori_loop(0, own_ref.shape[0], body, 0)


def tile_update(panels_ref, local, tile):
    left = jnp.concatenate([panels_ref[local + k] for k in range(KP)], axis=1)
    right = jnp.concatenate([tile(k) for k in range(KP)], axis=0)
    return jnp.dot(left, right, preferred_element_type=jnp.float32)


def start(*pairs):
    copies = [pltpu.make_async_copy(*pair) for pair in pairs]
    for copy in copies:
        copy.start()
    return copies


def load_level(offset, first_diag, sources, targets, arrived):
    from_hbm, panels_hbm, rights_hbm, diag_hbm = sources
    from_ref, panels_ref, rights_ref, diag_ref = targets
    copies = start(
        (from_hbm, from_ref, arrived.at[0]),
        (panels_hbm.at[pl.ds(offset, panels_ref.shape[0])], panels_ref, arrived.at[1]),
        (rights_hbm, rights_ref, arrived.at[2]),
        (diag_hbm.at[pl.ds(first_diag, TS)], diag_ref, arrived.at[3]),
    )
    for copy in copies:
        copy.wait()


def run_level(tile, panels_ref, rights_ref, diag_ref, rest_ref, solved_ref, sent_ref):
    for d in range(rights_ref.shape[0]):
        right = rights_ref[d] - tile_update(panels_ref, KP * d, lambda k: tile(KP * d + k))
        if d < TS:
            finish(right, diag_ref, d, solved_ref, sent_ref)
        else:
            rest_ref[d - TS] = right


def level_kernel(
    offset, first_diag, from_hbm, panels_hbm, rights_hbm, diag_hbm, received_ref,
    rest_ref, solved_ref, sent_ref, from_ref, panels_ref, rights_ref, diag_ref, arrived,
):
    load_level(
        offset, first_diag, (from_hbm, panels_hbm, rights_hbm, diag_hbm),
        (from_ref, panels_ref, rights_ref, diag_ref), arrived,
    )
    run_level(
        lambda e: received_ref[from_ref[offset + e]],
        panels_ref, rights_ref, diag_ref, rest_ref, solved_ref, sent_ref,
    )


def top_kernel(
    from_hbm, panels_hbm, rights_hbm, diag_hbm, at_ref, own_ref, other_ref,
    rest_ref, solved_ref, sent_ref, from_ref, panels_ref, rights_ref, diag_ref, arrived,
):
    load_level(
        0, TS, (from_hbm, panels_hbm, rights_hbm, diag_hbm),
        (from_ref, panels_ref, rights_ref, diag_ref), arrived,
    )
    run_level(
        lambda e: jnp.where(same_core(from_ref[e], at_ref), own_ref[e], other_ref[e]),
        panels_ref, rights_ref, diag_ref, rest_ref, solved_ref, sent_ref,
    )


def top_leaf_kernel(offset, from_ref, at_ref, own_ref, other_ref, panels_ref, right_ref, out_ref):
    first = offset + pl.program_id(0) * LEAF_STEP * KP

    def tile(entry):
        position = from_ref[entry]
        slot = position // (2 * SIDE) * SIDE + position % SIDE
        return jnp.where(same_core(position, at_ref), own_ref[slot], other_ref[slot])

    for d in range(LEAF_STEP):
        out_ref[d] = right_ref[d] - tile_update(
            panels_ref, KP * d, lambda k: tile(first + KP * d + k)
        )


def leaf_kernel(offset, from_ref, received_ref, panels_ref, right_ref, out_ref):
    first = offset + pl.program_id(0) * LEAF_STEP * KP
    for d in range(LEAF_STEP):
        out_ref[d] = right_ref[d] - tile_update(
            panels_ref, KP * d, lambda k: received_ref[from_ref[first + KP * d + k]]
        )


def last_kernel(
    offset, from_hbm, received_ref, panels_hbm, right_hbm, diag_hbm, out_hbm,
    from_ref, panels_ref, right_ref, diag_ref, out_ref, arrived, left,
):
    parts = TL // LAST_STEP
    [chosen] = start((from_hbm, from_ref, arrived.at[3 * parts]))
    loads = []
    for part in range(parts):
        first = part * LAST_STEP
        tiles = pl.ds(first, LAST_STEP)
        entries = pl.ds(KP * first, KP * LAST_STEP)
        loads.append(
            start(
                (
                    panels_hbm.at[pl.ds(offset + KP * first, KP * LAST_STEP)],
                    panels_ref.at[entries],
                    arrived.at[3 * part],
                ),
                (right_hbm.at[tiles], right_ref.at[tiles], arrived.at[3 * part + 1]),
                (
                    diag_hbm.at[pl.ds(LEVELS * TS + first, LAST_STEP)],
                    diag_ref.at[tiles],
                    arrived.at[3 * part + 2],
                ),
            )
        )
    chosen.wait()
    stores = []
    for part in range(parts):
        for copy in loads[part]:
            copy.wait()
        tiles = range(part * LAST_STEP, (part + 1) * LAST_STEP)
        rights = [
            right_ref[t]
            - tile_update(
                panels_ref, KP * t, lambda k: received_ref[from_ref[offset + KP * t + k]]
            )
            for t in tiles
        ]
        for t, right in zip(tiles, rights):
            out_ref[t] = solve(diag_ref[t], right)
        done = pl.ds(part * LAST_STEP, LAST_STEP)
        stores += start((out_ref.at[done], out_hbm.at[done], left.at[part]))
    for copy in stores:
        copy.wait()


def entries_block(offset, count):
    return pl.BlockSpec(
        (pl.Element(count), pl.Element(BS), pl.Element(BS)),
        lambda i, *_: (offset + i * count, 0, 0),
    )


def streamed(x):
    return pltpu.with_memory_space_constraint(x, pltpu.HBM)


def f32(*shape):
    return jax.ShapeDtypeStruct(shape, jnp.float32)


def b16(*shape):
    return jax.ShapeDtypeStruct(shape, jnp.bfloat16)


def leaf_pass(kernel, offset, scalars, received, stream, leaf_right):
    tiles, rows, rhs = leaf_right.shape
    return pl.pallas_call(
        kernel,
        grid_spec=pltpu.PrefetchScalarGridSpec(
            num_scalar_prefetch=len(scalars),
            grid=(tiles // LEAF_STEP,),
            in_specs=[whole()] * len(received)
            + [entries_block(offset, KP * LEAF_STEP), entries_block(0, LEAF_STEP)],
            out_specs=entries_block(0, LEAF_STEP),
        ),
        out_shape=pltpu.HBM((tiles, rows, rhs), jnp.float32),
        compiler_params=VMEM,
        name="leaf",
    )(*scalars, *received, stream, streamed(leaf_right))


def per_device(
    noise_parts, elimination_row, leaf_noise, diag_inverse, panels, panel_from, send_lists
):
    owners = lax.axis_size(AXES)
    rows = noise_parts.shape[0]
    rhs = noise_parts.shape[1]
    per_owner = rows // owners
    outgoing = pl.pallas_call(
        pack_kernel,
        out_shape=b16(owners, per_owner, 2 * rhs + BS),
        in_specs=[whole()] * 3,
        out_specs=whole(),
        compiler_params=VMEM,
        name="pack",
    )(elimination_row.reshape(1, rows), send_lists, noise_parts)
    arrived = lax.all_to_all(outgoing, AXES, 0, 0, tiled=True)
    send_row = send_lists[0]
    stream = streamed(panels)
    diag_stream = streamed(diag_inverse)
    from_stream = streamed(panel_from)
    solved, sent = pl.pallas_call(
        first_kernel,
        out_shape=(f32(TS, BS, rhs), b16(TS, BS, rhs)),
        in_specs=[whole(), in_hbm()],
        out_specs=(whole(), whole()),
        scratch_shapes=[pltpu.VMEM((TS, BS, BS), jnp.float32), pltpu.SemaphoreType.DMA],
        compiler_params=VMEM,
        name="first",
    )(arrived, diag_stream)
    rights, picks = pl.pallas_call(
        order_kernel,
        out_shape=(
            f32((LEVELS - 1) * TS, BS, rhs),
            jax.ShapeDtypeStruct((2, rows), jnp.int32),
        ),
        in_specs=[whole()],
        out_specs=(whole(), whole()),
        compiler_params=VMEM,
        name="order",
    )(arrived)
    in_smem = pl.BlockSpec(memory_space=pltpu.SMEM)
    leaf = lax.axis_index("leaf")
    at = jnp.stack([lax.axis_index("panel"), leaf // (2 * SIDE), leaf // 2 % SIDE, leaf % 2])
    near = KP * TS * (LEVELS - 1)
    mine = panel_from[:near]
    theirs = swap_core(mine)
    gathered = gather_core(sent)
    own, other = pl.pallas_call(
        near_kernel,
        out_shape=(b16(near, BS, rhs), b16(near, BS, rhs)),
        in_specs=[in_smem] * 4 + [whole()] * 3,
        out_specs=(whole(), whole()),
        compiler_params=VMEM,
        name="near",
    )(at, picks, mine, theirs, *gathered)
    other = swap_core(other)
    leaf_right = leaf_noise.reshape(TL, BS, rhs)
    all_solved = [solved]
    offset = 0
    send_offset = 0
    for tree_level in range(LEVELS):
        group = owners >> tree_level
        groups = [
            list(range(g * group, (g + 1) * group)) for g in range(owners // group)
        ]
        if tree_level:
            chosen = send_row[send_offset : send_offset + group]
            buffer = jnp.where((chosen == 0)[:, None, None], sent[0][None], sent[1][None])
            if tree_level == 1:
                gathered, buffer = lax.optimization_barrier((gathered, buffer))
                own_all, other_all = pl.pallas_call(
                    spread_kernel,
                    out_shape=(b16(owners // 2, BS, rhs), b16(owners // 2, BS, rhs)),
                    in_specs=[in_smem] * 2 + [whole()] * 3,
                    out_specs=(whole(), whole()),
                    compiler_params=VMEM,
                    name="spread",
                )(at, picks, *gathered)
                other_all = swap_core(other_all)
            received = lax.all_to_all(
                buffer, AXES, 0, 0, axis_index_groups=groups, tiled=True
            )
        if tree_level == 2:
            leaf_right = leaf_pass(
                functools.partial(top_leaf_kernel, KP * TS * (LEVELS - 1)),
                KP * TS * (LEVELS - 1),
                (panel_from, at),
                (own_all, other_all),
                stream,
                leaf_right,
            )
            leaf_right = leaf_pass(*waiting, leaf_right)
        if tree_level == 3:
            leaf_right = leaf_pass(*waiting, leaf_right)
        if tree_level >= 2:
            received, leaf_right = lax.optimization_barrier((received, leaf_right))
        send_offset += group
        sep_tiles = (LEVELS - 1 - tree_level) * TS
        leaf_offset = offset + KP * sep_tiles
        if tree_level < LEVELS - 1:
            operands = [from_stream, stream, streamed(rights), diag_stream]
            in_specs = [in_hbm()] * 4
            if tree_level:
                kernel = functools.partial(level_kernel, offset, (tree_level + 1) * TS)
                operands.append(received)
                in_specs.append(whole())
                waiting = (
                    functools.partial(leaf_kernel, leaf_offset),
                    leaf_offset,
                    (panel_from,),
                    (received,),
                    stream,
                )
            else:
                kernel = top_kernel
                operands += [at, own, other]
                in_specs += [in_smem, whole(), whole()]
            rights, solved, sent = pl.pallas_call(
                kernel,
                in_specs=in_specs,
                out_specs=(whole(),) * 3,
                out_shape=(
                    f32(max(sep_tiles - TS, TS), BS, rhs),
                    f32(TS, BS, rhs),
                    b16(TS, BS, rhs),
                ),
                scratch_shapes=[
                    pltpu.SMEM(panel_from.shape, jnp.int32),
                    pltpu.VMEM((KP * sep_tiles, BS, BS), jnp.bfloat16),
                    pltpu.VMEM((sep_tiles, BS, rhs), jnp.float32),
                    pltpu.VMEM((TS, BS, BS), jnp.float32),
                    pltpu.SemaphoreType.DMA((4,)),
                ],
                compiler_params=VMEM,
                name=f"level{tree_level}",
            )(*operands)
            all_solved.append(solved)
        else:
            parts = TL // LAST_STEP
            leaf_right = pl.pallas_call(
                functools.partial(last_kernel, leaf_offset),
                in_specs=[in_hbm(), whole()] + [in_hbm()] * 3,
                out_specs=in_hbm(),
                out_shape=pltpu.HBM((TL, BS, rhs), jnp.float32),
                scratch_shapes=[
                    pltpu.SMEM(panel_from.shape, jnp.int32),
                    pltpu.VMEM((KP * TL, BS, BS), jnp.bfloat16),
                    pltpu.VMEM((TL, BS, rhs), jnp.float32),
                    pltpu.VMEM((TL, BS, BS), jnp.float32),
                    pltpu.VMEM((TL, BS, rhs), jnp.float32),
                    pltpu.SemaphoreType.DMA((3 * parts + 1,)),
                    pltpu.SemaphoreType.DMA((parts,)),
                ],
                compiler_params=VMEM,
                name="last",
            )(from_stream, received, stream, streamed(leaf_right), diag_stream)
        offset = leaf_offset + KP * TL
    sep_solution = jnp.concatenate(all_solved, axis=0).reshape(rows, rhs)
    return (sep_solution, leaf_right.reshape(TL * BS, rhs))


def solution(mesh):
    return jax.shard_map(
        per_device,
        mesh=mesh,
        in_specs=(
            P(AXES, None),
            P(AXES),
            P(AXES, None),
            P(AXES, None, None),
            P(AXES, None, None),
            P(AXES),
            P(AXES, None),
        ),
        out_specs=(P(AXES, None), P(AXES, None)),
        check_vma=False,
    )
```

```python
import functools

import jax
import jax.numpy as jnp
from jax import lax
from jax.experimental import pallas as pl
from jax.experimental.pallas import tpu as pltpu
from jax.sharding import PartitionSpec as P

BS = 128
TS = 2
TL = 32
KP = 4
LEVELS = 4
AXES = ("leaf", "panel")
LEAF_STEP = 8
LAST_STEP = 8
SIDE = 4
CUTS = (0, 48, 96, 128)
ORDERS = ("xzy", "zyx", "yxz")
VMEM = pltpu.CompilerParams(vmem_limit_bytes=16 * 1024 * 1024)


def in_hbm():
    return pl.BlockSpec(memory_space=pltpu.HBM)


def whole():
    return pl.BlockSpec(memory_space=pltpu.VMEM)


def halves(x):
    high = x.astype(jnp.bfloat16)
    return high, (x - high.astype(jnp.float32)).astype(jnp.bfloat16)


def hot(condition):
    return condition.astype(jnp.float32).astype(jnp.bfloat16)


def transposed_dot(a, b):
    return lax.dot_general(a, b, (((1,), (1,)), ((), ())), preferred_element_type=jnp.float32)


def pack_kernel(target_ref, send_ref, noise_ref, out_ref):
    rows = noise_ref.shape[0]
    owners, per_owner, width = out_ref.shape
    target = target_ref[...]
    owner = target // rows
    slot = target % rows
    mine = owner == lax.broadcasted_iota(jnp.int32, (owners, rows), 0)
    before = lax.broadcasted_iota(jnp.int32, (rows, rows), 0) < lax.broadcasted_iota(
        jnp.int32, (rows, rows), 1
    )
    earlier = jnp.dot(hot(mine), hot(before), preferred_element_type=jnp.float32)
    rank = jnp.sum(jnp.where(mine, earlier, 0.0), axis=0, keepdims=True)
    position = owner * per_owner + rank.astype(jnp.int32)
    select = hot(position == lax.broadcasted_iota(jnp.int32, (rows, rows), 0))
    both = jnp.concatenate(halves(noise_ref[...]), axis=1)
    out = jnp.dot(select, both, preferred_element_type=jnp.float32)
    level_rows = TS * BS
    lane = lax.broadcasted_iota(jnp.int32, (BS, rows), 0)
    place = jnp.where(slot // level_rows == lane, slot % level_rows, -1)
    row = lax.broadcasted_iota(jnp.int32, (BS, owners), 0)
    picks = send_ref[:, :owners]
    theirs = (owner ^ SIDE) == lax.broadcasted_iota(jnp.int32, (owners, rows), 0)
    picked = jnp.dot(
        hot((picks > 0) & (row == LEVELS)), hot(mine), preferred_element_type=jnp.float32
    ) + jnp.dot(
        hot((picks > 0) & (row == LEVELS + 1)), hot(theirs), preferred_element_type=jnp.float32
    )
    place = jnp.where(lane < LEVELS, place.astype(jnp.float32), picked)
    meta = transposed_dot(select, place.astype(jnp.bfloat16))
    out = jnp.concatenate([out, meta], axis=1)
    out_ref[...] = out.reshape(owners, per_owner, width).astype(jnp.bfloat16)


def arrived_parts(arrived_ref):
    owners, per_owner, width = arrived_ref.shape
    rows = owners * per_owner
    arrived = arrived_ref[...].astype(jnp.float32).reshape(rows, width).astype(jnp.bfloat16)
    unit = hot(
        lax.broadcasted_iota(jnp.int32, (8, BS), 0) == lax.broadcasted_iota(jnp.int32, (8, BS), 1)
    )
    places = transposed_dot(unit, arrived[:, width - BS :]).astype(jnp.int32)
    return arrived[:, : width - BS], places


def order_rows(arrived, places, tree_level):
    rows, width = arrived.shape
    select = hot(
        places[tree_level : tree_level + 1]
        == lax.broadcasted_iota(jnp.int32, (TS * BS, rows), 0)
    )
    both = jnp.dot(select, arrived, preferred_element_type=jnp.float32)
    return both[:, : width // 2] + both[:, width // 2 :]


def solve(diag, right):
    left = jnp.concatenate(halves(diag), axis=0)
    both = jnp.concatenate(halves(right), axis=1)
    out = jnp.dot(left, both, preferred_element_type=jnp.float32)
    rows, width = diag.shape[0], right.shape[1]
    return (
        out[:rows, :width]
        + (out[:rows, width:] + out[rows:, :width])
        + out[rows:, width:]
    )


def finish(right, diag_ref, t, solved_ref, sent_ref):
    solved = solve(diag_ref[t], right)
    solved_ref[t] = solved
    sent_ref[t] = solved.astype(jnp.bfloat16)


def first_kernel(arrived_ref, diag_hbm, solved_ref, sent_ref, diag_ref, arrived):
    fetch = pltpu.make_async_copy(diag_hbm.at[pl.ds(0, TS)], diag_ref, arrived)
    fetch.start()
    right = order_rows(*arrived_parts(arrived_ref), 0)
    fetch.wait()
    for t in range(TS):
        finish(right[t * BS : (t + 1) * BS], diag_ref, t, solved_ref, sent_ref)


def order_kernel(arrived_ref, out_ref, picks_ref):
    arrived, places = arrived_parts(arrived_ref)
    for i in range(LEVELS - 1):
        right = order_rows(arrived, places, i + 1)
        for t in range(TS):
            out_ref[i * TS + t] = right[t * BS : (t + 1) * BS]
    picks_ref[...] = places[LEVELS : LEVELS + 2]


def step_pairs(axis, second):
    pairs = []
    for device in range(2 * SIDE**3):
        at = {
            "x": device % SIDE,
            "c": device // SIDE % 2,
            "z": device // (2 * SIDE) % SIDE,
            "y": device // (2 * SIDE * SIDE),
        }
        up = (at[axis] + at["c"] + second) % 2 == 0
        at[axis] = (at[axis] + (1 if up else -1)) % SIDE
        pairs.append((device, ((at["y"] * SIDE + at["z"]) * 2 + at["c"]) * SIDE + at["x"]))
    return pairs


def gather_core(sent, early):
    sent, early = lax.optimization_barrier((sent, early))
    parts = [sent[:, a:b] for a, b in zip(CUTS, CUTS[1:])]
    steps = 2 * len(ORDERS[0])
    for step in range(steps):
        arriving = [
            lax.ppermute(part, AXES, step_pairs(order[step // 2], step % 2))
            for part, order in zip(parts, ORDERS)
        ]
        if step == 0:
            early = swap_core(early)
            early, arriving[2] = lax.optimization_barrier((early, arriving[2]))
        if step < steps - 1:
            parts = [
                lax.optimization_barrier(jnp.concatenate(both, axis=0))
                for both in zip(parts, arriving)
            ]
    return [x for both in zip(parts, arriving) for x in both], early


def swap_core(x):
    return lax.ppermute(x, AXES, [(i, i ^ SIDE) for i in range(2 * SIDE**3)])


def same_core(position, at_ref):
    return (position // SIDE) % 2 == at_ref[3]


def take(parts, at_ref, position, pick):
    core = at_ref[3]

    def place(axis, there):
        here = at_ref["xyz".index(axis)]
        away = there - here
        away = jnp.where((here + core) % 2 == 0, away, -away) & (SIDE - 1)
        return away ^ (away >> 1)

    there = {
        "x": position % SIDE,
        "z": position // (2 * SIDE) % SIDE,
        "y": position // (2 * SIDE * SIDE),
    }
    spots = {axis: place(axis, there[axis]) for axis in there}
    for held, came, order in zip(parts[::2], parts[1::2], ORDERS):
        at = 0
        for axis in reversed(order):
            at = at * SIDE + spots[axis]
        at = at * TS + pick
        half = held.shape[0]
        yield jnp.where(at < half, held[at & (half - 1)], came[at & (half - 1)])


def near_kernel(which, at_ref, picks_ref, from_ref, *refs):
    *parts, out_ref = refs
    for e in range(out_ref.shape[0]):
        position = from_ref[e]
        blocks = take(parts, at_ref, position, picks_ref[which, position * 8])
        for first, block in zip(CUTS, blocks):
            out_ref[e, first : first + block.shape[0]] = block


def spread_kernel(at_ref, picks_ref, *refs):
    *parts, own_ref, other_ref = refs

    def body(i, carry):
        position = i // SIDE * (2 * SIDE) + at_ref[3] * SIDE + i % SIDE
        for which, out_ref in enumerate((own_ref, other_ref)):
            blocks = take(parts, at_ref, position, picks_ref[which, position * 8])
            for first, block in zip(CUTS, blocks):
                out_ref[i, first : first + block.shape[0]] = block
        return carry

    lax.fori_loop(0, own_ref.shape[0], body, 0)


def tile_update(panels_ref, local, tile):
    left = jnp.concatenate([panels_ref[local + k] for k in range(KP)], axis=1)
    right = jnp.concatenate([tile(k) for k in range(KP)], axis=0)
    return jnp.dot(left, right, preferred_element_type=jnp.float32)


def start(*pairs):
    copies = [pltpu.make_async_copy(*pair) for pair in pairs]
    for copy in copies:
        copy.start()
    return copies


def load_level(offset, first_diag, sources, targets, arrived):
    from_hbm, panels_hbm, rights_hbm, diag_hbm = sources
    from_ref, panels_ref, rights_ref, diag_ref = targets
    copies = start(
        (from_hbm, from_ref, arrived.at[0]),
        (panels_hbm.at[pl.ds(offset, panels_ref.shape[0])], panels_ref, arrived.at[1]),
        (rights_hbm, rights_ref, arrived.at[2]),
        (diag_hbm.at[pl.ds(first_diag, TS)], diag_ref, arrived.at[3]),
    )
    for copy in copies:
        copy.wait()


def run_level(tile, panels_ref, rights_ref, diag_ref, rest_ref, solved_ref, sent_ref):
    for d in range(rights_ref.shape[0]):
        right = rights_ref[d] - tile_update(panels_ref, KP * d, lambda k: tile(KP * d + k))
        if d < TS:
            finish(right, diag_ref, d, solved_ref, sent_ref)
        else:
            rest_ref[d - TS] = right


def level_kernel(
    offset, first_diag, from_hbm, panels_hbm, rights_hbm, diag_hbm, received_ref,
    rest_ref, solved_ref, sent_ref, from_ref, panels_ref, rights_ref, diag_ref, arrived,
):
    load_level(
        offset, first_diag, (from_hbm, panels_hbm, rights_hbm, diag_hbm),
        (from_ref, panels_ref, rights_ref, diag_ref), arrived,
    )
    run_level(
        lambda e: received_ref[from_ref[offset + e]],
        panels_ref, rights_ref, diag_ref, rest_ref, solved_ref, sent_ref,
    )


def top_kernel(
    from_hbm, panels_hbm, rights_hbm, diag_hbm, at_ref, own_ref, other_ref,
    rest_ref, solved_ref, sent_ref, from_ref, panels_ref, rights_ref, diag_ref, arrived,
):
    load_level(
        0, TS, (from_hbm, panels_hbm, rights_hbm, diag_hbm),
        (from_ref, panels_ref, rights_ref, diag_ref), arrived,
    )
    run_level(
        lambda e: jnp.where(same_core(from_ref[e], at_ref), own_ref[e], other_ref[e]),
        panels_ref, rights_ref, diag_ref, rest_ref, solved_ref, sent_ref,
    )


def top_leaf_kernel(offset, from_ref, at_ref, own_ref, other_ref, panels_ref, right_ref, out_ref):
    first = offset + pl.program_id(0) * LEAF_STEP * KP

    def tile(entry):
        position = from_ref[entry]
        slot = position // (2 * SIDE) * SIDE + position % SIDE
        return jnp.where(same_core(position, at_ref), own_ref[slot], other_ref[slot])

    for d in range(LEAF_STEP):
        out_ref[d] = right_ref[d] - tile_update(
            panels_ref, KP * d, lambda k: tile(first + KP * d + k)
        )


def leaf_kernel(offset, from_ref, received_ref, panels_ref, right_ref, out_ref):
    first = offset + pl.program_id(0) * LEAF_STEP * KP
    for d in range(LEAF_STEP):
        out_ref[d] = right_ref[d] - tile_update(
            panels_ref, KP * d, lambda k: received_ref[from_ref[first + KP * d + k]]
        )


def last_kernel(
    offset, from_hbm, received_ref, panels_hbm, right_hbm, diag_hbm, out_hbm,
    from_ref, panels_ref, right_ref, diag_ref, out_ref, arrived, left,
):
    parts = TL // LAST_STEP
    [chosen] = start((from_hbm, from_ref, arrived.at[3 * parts]))
    loads = []
    for part in range(parts):
        first = part * LAST_STEP
        tiles = pl.ds(first, LAST_STEP)
        entries = pl.ds(KP * first, KP * LAST_STEP)
        loads.append(
            start(
                (
                    panels_hbm.at[pl.ds(offset + KP * first, KP * LAST_STEP)],
                    panels_ref.at[entries],
                    arrived.at[3 * part],
                ),
                (right_hbm.at[tiles], right_ref.at[tiles], arrived.at[3 * part + 1]),
                (
                    diag_hbm.at[pl.ds(LEVELS * TS + first, LAST_STEP)],
                    diag_ref.at[tiles],
                    arrived.at[3 * part + 2],
                ),
            )
        )
    chosen.wait()
    stores = []
    for part in range(parts):
        for copy in loads[part]:
            copy.wait()
        tiles = range(part * LAST_STEP, (part + 1) * LAST_STEP)
        rights = [
            right_ref[t]
            - tile_update(
                panels_ref, KP * t, lambda k: received_ref[from_ref[offset + KP * t + k]]
            )
            for t in tiles
        ]
        for t, right in zip(tiles, rights):
            out_ref[t] = solve(diag_ref[t], right)
        done = pl.ds(part * LAST_STEP, LAST_STEP)
        stores += start((out_ref.at[done], out_hbm.at[done], left.at[part]))
    for copy in stores:
        copy.wait()


def entries_block(offset, count):
    return pl.BlockSpec(
        (pl.Element(count), pl.Element(BS), pl.Element(BS)),
        lambda i, *_: (offset + i * count, 0, 0),
    )


def streamed(x):
    return pltpu.with_memory_space_constraint(x, pltpu.HBM)


def f32(*shape):
    return jax.ShapeDtypeStruct(shape, jnp.float32)


def b16(*shape):
    return jax.ShapeDtypeStruct(shape, jnp.bfloat16)


def leaf_pass(kernel, offset, scalars, received, stream, leaf_right):
    tiles, rows, rhs = leaf_right.shape
    return pl.pallas_call(
        kernel,
        grid_spec=pltpu.PrefetchScalarGridSpec(
            num_scalar_prefetch=len(scalars),
            grid=(tiles // LEAF_STEP,),
            in_specs=[whole()] * len(received)
            + [entries_block(offset, KP * LEAF_STEP), entries_block(0, LEAF_STEP)],
            out_specs=entries_block(0, LEAF_STEP),
        ),
        out_shape=pltpu.HBM((tiles, rows, rhs), jnp.float32),
        compiler_params=VMEM,
        name="leaf",
    )(*scalars, *received, stream, streamed(leaf_right))


def per_device(
    noise_parts, elimination_row, leaf_noise, diag_inverse, panels, panel_from, send_lists
):
    owners = lax.axis_size(AXES)
    rows = noise_parts.shape[0]
    rhs = noise_parts.shape[1]
    per_owner = rows // owners
    outgoing = pl.pallas_call(
        pack_kernel,
        out_shape=b16(owners, per_owner, 2 * rhs + BS),
        in_specs=[whole()] * 3,
        out_specs=whole(),
        compiler_params=VMEM,
        name="pack",
    )(elimination_row.reshape(1, rows), send_lists, noise_parts)
    arrived = lax.all_to_all(outgoing, AXES, 0, 0, tiled=True)
    send_row = send_lists[0]
    stream = streamed(panels)
    diag_stream = streamed(diag_inverse)
    from_stream = streamed(panel_from)
    solved, sent = pl.pallas_call(
        first_kernel,
        out_shape=(f32(TS, BS, rhs), b16(TS, BS, rhs)),
        in_specs=[whole(), in_hbm()],
        out_specs=(whole(), whole()),
        scratch_shapes=[pltpu.VMEM((TS, BS, BS), jnp.float32), pltpu.SemaphoreType.DMA],
        compiler_params=VMEM,
        name="first",
    )(arrived, diag_stream)
    rights, picks = pl.pallas_call(
        order_kernel,
        out_shape=(
            f32((LEVELS - 1) * TS, BS, rhs),
            jax.ShapeDtypeStruct((2, rows), jnp.int32),
        ),
        in_specs=[whole()],
        out_specs=(whole(), whole()),
        compiler_params=VMEM,
        name="order",
    )(arrived)
    in_smem = pl.BlockSpec(memory_space=pltpu.SMEM)
    leaf = lax.axis_index("leaf")
    at = jnp.stack([lax.axis_index("panel"), leaf // (2 * SIDE), leaf // 2 % SIDE, leaf % 2])
    near = KP * TS * (LEVELS - 1)
    mine = panel_from[:near]
    gathered, theirs = gather_core(sent, mine)
    near_tiles = [
        pl.pallas_call(
            functools.partial(near_kernel, which),
            out_shape=b16(near, BS, rhs),
            in_specs=[in_smem] * 3 + [whole()] * 6,
            out_specs=whole(),
            compiler_params=VMEM,
            name=f"near{which}",
        )(at, picks, wanted, *gathered)
        for which, wanted in enumerate((mine, theirs))
    ]
    own, other = near_tiles[0], swap_core(near_tiles[1])
    leaf_right = leaf_noise.reshape(TL, BS, rhs)
    all_solved = [solved]
    offset = 0
    send_offset = 0
    for tree_level in range(LEVELS):
        group = owners >> tree_level
        groups = [
            list(range(g * group, (g + 1) * group)) for g in range(owners // group)
        ]
        if tree_level:
            chosen = send_row[send_offset : send_offset + group]
            buffer = jnp.where((chosen == 0)[:, None, None], sent[0][None], sent[1][None])
            if tree_level == 1:
                gathered, buffer = lax.optimization_barrier((gathered, buffer))
                own_all, other_all = pl.pallas_call(
                    spread_kernel,
                    out_shape=(b16(owners // 2, BS, rhs), b16(owners // 2, BS, rhs)),
                    in_specs=[in_smem] * 2 + [whole()] * 6,
                    out_specs=(whole(), whole()),
                    compiler_params=VMEM,
                    name="spread",
                )(at, picks, *gathered)
                other_all = swap_core(other_all)
            received = lax.all_to_all(
                buffer, AXES, 0, 0, axis_index_groups=groups, tiled=True
            )
        if tree_level == 2:
            leaf_right = leaf_pass(
                functools.partial(top_leaf_kernel, KP * TS * (LEVELS - 1)),
                KP * TS * (LEVELS - 1),
                (panel_from, at),
                (own_all, other_all),
                stream,
                leaf_right,
            )
            leaf_right = leaf_pass(*waiting, leaf_right)
        if tree_level == 3:
            leaf_right = leaf_pass(*waiting, leaf_right)
        if tree_level >= 2:
            received, leaf_right = lax.optimization_barrier((received, leaf_right))
        send_offset += group
        sep_tiles = (LEVELS - 1 - tree_level) * TS
        leaf_offset = offset + KP * sep_tiles
        if tree_level < LEVELS - 1:
            operands = [from_stream, stream, streamed(rights), diag_stream]
            in_specs = [in_hbm()] * 4
            if tree_level:
                kernel = functools.partial(level_kernel, offset, (tree_level + 1) * TS)
                operands.append(received)
                in_specs.append(whole())
                waiting = (
                    functools.partial(leaf_kernel, leaf_offset),
                    leaf_offset,
                    (panel_from,),
                    (received,),
                    stream,
                )
            else:
                kernel = top_kernel
                operands += [at, own, other]
                in_specs += [in_smem, whole(), whole()]
            rights, solved, sent = pl.pallas_call(
                kernel,
                in_specs=in_specs,
                out_specs=(whole(),) * 3,
                out_shape=(
                    f32(max(sep_tiles - TS, TS), BS, rhs),
                    f32(TS, BS, rhs),
                    b16(TS, BS, rhs),
                ),
                scratch_shapes=[
                    pltpu.SMEM(panel_from.shape, jnp.int32),
                    pltpu.VMEM((KP * sep_tiles, BS, BS), jnp.bfloat16),
                    pltpu.VMEM((sep_tiles, BS, rhs), jnp.float32),
                    pltpu.VMEM((TS, BS, BS), jnp.float32),
                    pltpu.SemaphoreType.DMA((4,)),
                ],
                compiler_params=VMEM,
                name=f"level{tree_level}",
            )(*operands)
            all_solved.append(solved)
        else:
            parts = TL // LAST_STEP
            leaf_right = pl.pallas_call(
                functools.partial(last_kernel, leaf_offset),
                in_specs=[in_hbm(), whole()] + [in_hbm()] * 3,
                out_specs=in_hbm(),
                out_shape=pltpu.HBM((TL, BS, rhs), jnp.float32),
                scratch_shapes=[
                    pltpu.SMEM(panel_from.shape, jnp.int32),
                    pltpu.VMEM((KP * TL, BS, BS), jnp.bfloat16),
                    pltpu.VMEM((TL, BS, rhs), jnp.float32),
                    pltpu.VMEM((TL, BS, BS), jnp.float32),
                    pltpu.VMEM((TL, BS, rhs), jnp.float32),
                    pltpu.SemaphoreType.DMA((3 * parts + 1,)),
                    pltpu.SemaphoreType.DMA((parts,)),
                ],
                compiler_params=VMEM,
                name="last",
            )(from_stream, received, stream, streamed(leaf_right), diag_stream)
        offset = leaf_offset + KP * TL
    sep_solution = jnp.concatenate(all_solved, axis=0).reshape(rows, rhs)
    return (sep_solution, leaf_right.reshape(TL * BS, rhs))


def solution(mesh):
    return jax.shard_map(
        per_device,
        mesh=mesh,
        in_specs=(
            P(AXES, None),
            P(AXES),
            P(AXES, None),
            P(AXES, None, None),
            P(AXES, None, None),
            P(AXES),
            P(AXES, None),
        ),
        out_specs=(P(AXES, None), P(AXES, None)),
        check_vma=False,
    )
```

```python
import functools

import jax
import jax.numpy as jnp
from jax import lax
from jax.experimental import pallas as pl
from jax.experimental.pallas import tpu as pltpu
from jax.sharding import PartitionSpec as P

BS = 128
TS = 2
TL = 32
KP = 4
LEVELS = 4
AXES = ("leaf", "panel")
LEAF_STEP = 8
LAST_STEP = 8
SIDE = 4
CUTS = (0, 48, 96, 128)
ORDERS = ("xzy", "zyx", "yxz")
VMEM = pltpu.CompilerParams(vmem_limit_bytes=16 * 1024 * 1024)


def in_hbm():
    return pl.BlockSpec(memory_space=pltpu.HBM)


def whole():
    return pl.BlockSpec(memory_space=pltpu.VMEM)


def halves(x):
    high = x.astype(jnp.bfloat16)
    return high, (x - high.astype(jnp.float32)).astype(jnp.bfloat16)


def hot(condition):
    return condition.astype(jnp.float32).astype(jnp.bfloat16)


def transposed_dot(a, b):
    return lax.dot_general(a, b, (((1,), (1,)), ((), ())), preferred_element_type=jnp.float32)


def pack_kernel(
    target_hbm, send_hbm, noise_hbm, out_ref, target_ref, send_ref, noise_ref, arrived
):
    rows = noise_ref.shape[0]
    owners, per_owner, width = out_ref.shape
    *lists, noise = start(
        (target_hbm, target_ref, arrived.at[0]),
        (send_hbm, send_ref, arrived.at[1]),
        (noise_hbm, noise_ref, arrived.at[2]),
    )
    for copy in lists:
        copy.wait()
    target = target_ref[...]
    owner = target // rows
    slot = target % rows
    mine = owner == lax.broadcasted_iota(jnp.int32, (owners, rows), 0)
    before = lax.broadcasted_iota(jnp.int32, (rows, rows), 0) < lax.broadcasted_iota(
        jnp.int32, (rows, rows), 1
    )
    earlier = jnp.dot(hot(mine), hot(before), preferred_element_type=jnp.float32)
    rank = jnp.sum(jnp.where(mine, earlier, 0.0), axis=0, keepdims=True)
    position = owner * per_owner + rank.astype(jnp.int32)
    select = hot(position == lax.broadcasted_iota(jnp.int32, (rows, rows), 0))
    noise.wait()
    both = jnp.concatenate(halves(noise_ref[...]), axis=1)
    out = jnp.dot(select, both, preferred_element_type=jnp.float32)
    level_rows = TS * BS
    lane = lax.broadcasted_iota(jnp.int32, (BS, rows), 0)
    place = jnp.where(slot // level_rows == lane, slot % level_rows, -1)
    row = lax.broadcasted_iota(jnp.int32, (BS, owners), 0)
    picks = send_ref[:, :owners]
    theirs = (owner ^ SIDE) == lax.broadcasted_iota(jnp.int32, (owners, rows), 0)
    picked = jnp.dot(
        hot((picks > 0) & (row == LEVELS)), hot(mine), preferred_element_type=jnp.float32
    ) + jnp.dot(
        hot((picks > 0) & (row == LEVELS + 1)), hot(theirs), preferred_element_type=jnp.float32
    )
    place = jnp.where(lane < LEVELS, place.astype(jnp.float32), picked)
    meta = transposed_dot(select, place.astype(jnp.bfloat16))
    out = jnp.concatenate([out, meta], axis=1)
    out_ref[...] = out.reshape(owners, per_owner, width).astype(jnp.bfloat16)


def arrived_parts(arrived_ref):
    owners, per_owner, width = arrived_ref.shape
    rows = owners * per_owner
    arrived = arrived_ref[...].astype(jnp.float32).reshape(rows, width).astype(jnp.bfloat16)
    unit = hot(
        lax.broadcasted_iota(jnp.int32, (8, BS), 0) == lax.broadcasted_iota(jnp.int32, (8, BS), 1)
    )
    places = transposed_dot(unit, arrived[:, width - BS :]).astype(jnp.int32)
    return arrived[:, : width - BS], places


def order_rows(arrived, places, tree_level):
    rows, width = arrived.shape
    select = hot(
        places[tree_level : tree_level + 1]
        == lax.broadcasted_iota(jnp.int32, (TS * BS, rows), 0)
    )
    both = jnp.dot(select, arrived, preferred_element_type=jnp.float32)
    return both[:, : width // 2] + both[:, width // 2 :]


def solve(diag, right):
    left = jnp.concatenate(halves(diag), axis=0)
    both = jnp.concatenate(halves(right), axis=1)
    out = jnp.dot(left, both, preferred_element_type=jnp.float32)
    rows, width = diag.shape[0], right.shape[1]
    return (
        out[:rows, :width]
        + (out[:rows, width:] + out[rows:, :width])
        + out[rows:, width:]
    )


def finish(right, diag_ref, t, solved_ref, sent_ref):
    solved = solve(diag_ref[t], right)
    solved_ref[t] = solved
    sent_ref[t] = solved.astype(jnp.bfloat16)


def first_kernel(arrived_ref, diag_hbm, solved_ref, sent_ref, diag_ref, arrived):
    fetch = pltpu.make_async_copy(diag_hbm.at[pl.ds(0, TS)], diag_ref, arrived)
    fetch.start()
    right = order_rows(*arrived_parts(arrived_ref), 0)
    fetch.wait()
    for t in range(TS):
        finish(right[t * BS : (t + 1) * BS], diag_ref, t, solved_ref, sent_ref)


def order_kernel(arrived_ref, out_ref, picks_ref):
    arrived, places = arrived_parts(arrived_ref)
    for i in range(LEVELS - 1):
        right = order_rows(arrived, places, i + 1)
        for t in range(TS):
            out_ref[i * TS + t] = right[t * BS : (t + 1) * BS]
    picks_ref[...] = places[LEVELS : LEVELS + 2]


def step_pairs(axis, second):
    pairs = []
    for device in range(2 * SIDE**3):
        at = {
            "x": device % SIDE,
            "c": device // SIDE % 2,
            "z": device // (2 * SIDE) % SIDE,
            "y": device // (2 * SIDE * SIDE),
        }
        up = (at[axis] + at["c"] + second) % 2 == 0
        at[axis] = (at[axis] + (1 if up else -1)) % SIDE
        pairs.append((device, ((at["y"] * SIDE + at["z"]) * 2 + at["c"]) * SIDE + at["x"]))
    return pairs


def gather_core(sent, early):
    sent, early = lax.optimization_barrier((sent, early))
    parts = [sent[:, a:b] for a, b in zip(CUTS, CUTS[1:])]
    steps = 2 * len(ORDERS[0])
    for step in range(steps):
        arriving = [
            lax.ppermute(part, AXES, step_pairs(order[step // 2], step % 2))
            for part, order in zip(parts, ORDERS)
        ]
        if step == 0:
            early = swap_core(early)
            early, arriving[2] = lax.optimization_barrier((early, arriving[2]))
        if step < steps - 1:
            parts = [
                lax.optimization_barrier(jnp.concatenate(both, axis=0))
                for both in zip(parts, arriving)
            ]
    return [x for both in zip(parts, arriving) for x in both], early


def swap_core(x):
    return lax.ppermute(x, AXES, [(i, i ^ SIDE) for i in range(2 * SIDE**3)])


def same_core(position, at_ref):
    return (position // SIDE) % 2 == at_ref[3]


def take(parts, at_ref, position, pick):
    core = at_ref[3]

    def place(axis, there):
        here = at_ref["xyz".index(axis)]
        away = there - here
        away = jnp.where((here + core) % 2 == 0, away, -away) & (SIDE - 1)
        return away ^ (away >> 1)

    there = {
        "x": position % SIDE,
        "z": position // (2 * SIDE) % SIDE,
        "y": position // (2 * SIDE * SIDE),
    }
    spots = {axis: place(axis, there[axis]) for axis in there}
    for held, came, order in zip(parts[::2], parts[1::2], ORDERS):
        at = 0
        for axis in reversed(order):
            at = at * SIDE + spots[axis]
        at = at * TS + pick
        half = held.shape[0]
        yield jnp.where(at < half, held[at & (half - 1)], came[at & (half - 1)])


def near_kernel(which, at_ref, picks_ref, from_ref, *refs):
    *parts, out_ref = refs
    for e in range(out_ref.shape[0]):
        position = from_ref[e]
        blocks = take(parts, at_ref, position, picks_ref[which, position * 8])
        for first, block in zip(CUTS, blocks):
            out_ref[e, first : first + block.shape[0]] = block


def spread_kernel(at_ref, picks_ref, *refs):
    *parts, own_ref, other_ref = refs

    def body(i, carry):
        position = i // SIDE * (2 * SIDE) + at_ref[3] * SIDE + i % SIDE
        for which, out_ref in enumerate((own_ref, other_ref)):
            blocks = take(parts, at_ref, position, picks_ref[which, position * 8])
            for first, block in zip(CUTS, blocks):
                out_ref[i, first : first + block.shape[0]] = block
        return carry

    lax.fori_loop(0, own_ref.shape[0], body, 0)


def tile_update(panels_ref, local, tile):
    left = jnp.concatenate([panels_ref[local + k] for k in range(KP)], axis=1)
    right = jnp.concatenate([tile(k) for k in range(KP)], axis=0)
    return jnp.dot(left, right, preferred_element_type=jnp.float32)


def start(*pairs):
    copies = [pltpu.make_async_copy(*pair) for pair in pairs]
    for copy in copies:
        copy.start()
    return copies


def load_level(offset, first_diag, sources, targets, arrived):
    from_hbm, panels_hbm, rights_hbm, diag_hbm = sources
    from_ref, panels_ref, rights_ref, diag_ref = targets
    copies = start(
        (from_hbm, from_ref, arrived.at[0]),
        (panels_hbm.at[pl.ds(offset, panels_ref.shape[0])], panels_ref, arrived.at[1]),
        (rights_hbm, rights_ref, arrived.at[2]),
        (diag_hbm.at[pl.ds(first_diag, TS)], diag_ref, arrived.at[3]),
    )
    for copy in copies:
        copy.wait()


def run_level(tile, panels_ref, rights_ref, diag_ref, rest_ref, solved_ref, sent_ref):
    for d in range(rights_ref.shape[0]):
        right = rights_ref[d] - tile_update(panels_ref, KP * d, lambda k: tile(KP * d + k))
        if d < TS:
            finish(right, diag_ref, d, solved_ref, sent_ref)
        else:
            rest_ref[d - TS] = right


def level_kernel(
    offset, first_diag, from_hbm, panels_hbm, rights_hbm, diag_hbm, received_ref,
    rest_ref, solved_ref, sent_ref, from_ref, panels_ref, rights_ref, diag_ref, arrived,
):
    load_level(
        offset, first_diag, (from_hbm, panels_hbm, rights_hbm, diag_hbm),
        (from_ref, panels_ref, rights_ref, diag_ref), arrived,
    )
    run_level(
        lambda e: received_ref[from_ref[offset + e]],
        panels_ref, rights_ref, diag_ref, rest_ref, solved_ref, sent_ref,
    )


def top_kernel(
    from_hbm, panels_hbm, rights_hbm, diag_hbm, at_ref, own_ref, other_ref,
    rest_ref, solved_ref, sent_ref, from_ref, panels_ref, rights_ref, diag_ref, arrived,
):
    load_level(
        0, TS, (from_hbm, panels_hbm, rights_hbm, diag_hbm),
        (from_ref, panels_ref, rights_ref, diag_ref), arrived,
    )
    run_level(
        lambda e: jnp.where(same_core(from_ref[e], at_ref), own_ref[e], other_ref[e]),
        panels_ref, rights_ref, diag_ref, rest_ref, solved_ref, sent_ref,
    )


def top_leaf_kernel(offset, from_ref, at_ref, own_ref, other_ref, panels_ref, right_ref, out_ref):
    first = offset + pl.program_id(0) * LEAF_STEP * KP

    def tile(entry):
        position = from_ref[entry]
        slot = position // (2 * SIDE) * SIDE + position % SIDE
        return jnp.where(same_core(position, at_ref), own_ref[slot], other_ref[slot])

    for d in range(LEAF_STEP):
        out_ref[d] = right_ref[d] - tile_update(
            panels_ref, KP * d, lambda k: tile(first + KP * d + k)
        )


def leaf_kernel(offset, from_ref, received_ref, panels_ref, right_ref, out_ref):
    first = offset + pl.program_id(0) * LEAF_STEP * KP
    for d in range(LEAF_STEP):
        out_ref[d] = right_ref[d] - tile_update(
            panels_ref, KP * d, lambda k: received_ref[from_ref[first + KP * d + k]]
        )


def last_kernel(
    offset, from_hbm, received_ref, panels_hbm, right_hbm, diag_hbm, out_hbm,
    from_ref, panels_ref, right_ref, diag_ref, out_ref, arrived, left,
):
    parts = TL // LAST_STEP
    [chosen] = start((from_hbm, from_ref, arrived.at[3 * parts]))
    loads = []
    for part in range(parts):
        first = part * LAST_STEP
        tiles = pl.ds(first, LAST_STEP)
        entries = pl.ds(KP * first, KP * LAST_STEP)
        loads.append(
            start(
                (
                    panels_hbm.at[pl.ds(offset + KP * first, KP * LAST_STEP)],
                    panels_ref.at[entries],
                    arrived.at[3 * part],
                ),
                (right_hbm.at[tiles], right_ref.at[tiles], arrived.at[3 * part + 1]),
                (
                    diag_hbm.at[pl.ds(LEVELS * TS + first, LAST_STEP)],
                    diag_ref.at[tiles],
                    arrived.at[3 * part + 2],
                ),
            )
        )
    chosen.wait()
    stores = []
    for part in range(parts):
        for copy in loads[part]:
            copy.wait()
        tiles = range(part * LAST_STEP, (part + 1) * LAST_STEP)
        rights = [
            right_ref[t]
            - tile_update(
                panels_ref, KP * t, lambda k: received_ref[from_ref[offset + KP * t + k]]
            )
            for t in tiles
        ]
        for t, right in zip(tiles, rights):
            out_ref[t] = solve(diag_ref[t], right)
        done = pl.ds(part * LAST_STEP, LAST_STEP)
        stores += start((out_ref.at[done], out_hbm.at[done], left.at[part]))
    for copy in stores:
        copy.wait()


def entries_block(offset, count):
    return pl.BlockSpec(
        (pl.Element(count), pl.Element(BS), pl.Element(BS)),
        lambda i, *_: (offset + i * count, 0, 0),
    )


def streamed(x):
    return pltpu.with_memory_space_constraint(x, pltpu.HBM)


def f32(*shape):
    return jax.ShapeDtypeStruct(shape, jnp.float32)


def b16(*shape):
    return jax.ShapeDtypeStruct(shape, jnp.bfloat16)


def leaf_pass(kernel, offset, scalars, received, stream, leaf_right):
    tiles, rows, rhs = leaf_right.shape
    return pl.pallas_call(
        kernel,
        grid_spec=pltpu.PrefetchScalarGridSpec(
            num_scalar_prefetch=len(scalars),
            grid=(tiles // LEAF_STEP,),
            in_specs=[whole()] * len(received)
            + [entries_block(offset, KP * LEAF_STEP), entries_block(0, LEAF_STEP)],
            out_specs=entries_block(0, LEAF_STEP),
        ),
        out_shape=pltpu.HBM((tiles, rows, rhs), jnp.float32),
        compiler_params=VMEM,
        name="leaf",
    )(*scalars, *received, stream, streamed(leaf_right))


def per_device(
    noise_parts, elimination_row, leaf_noise, diag_inverse, panels, panel_from, send_lists
):
    owners = lax.axis_size(AXES)
    rows = noise_parts.shape[0]
    rhs = noise_parts.shape[1]
    per_owner = rows // owners
    outgoing = pl.pallas_call(
        pack_kernel,
        out_shape=b16(owners, per_owner, 2 * rhs + BS),
        in_specs=[in_hbm()] * 3,
        out_specs=whole(),
        scratch_shapes=[
            pltpu.VMEM((1, rows), jnp.int32),
            pltpu.VMEM(send_lists.shape, jnp.int32),
            pltpu.VMEM((rows, rhs), jnp.float32),
            pltpu.SemaphoreType.DMA((3,)),
        ],
        compiler_params=VMEM,
        name="pack",
    )(*map(streamed, (elimination_row.reshape(1, rows), send_lists, noise_parts)))
    arrived = lax.all_to_all(outgoing, AXES, 0, 0, tiled=True)
    send_row = send_lists[0]
    stream = streamed(panels)
    diag_stream = streamed(diag_inverse)
    from_stream = streamed(panel_from)
    solved, sent = pl.pallas_call(
        first_kernel,
        out_shape=(f32(TS, BS, rhs), b16(TS, BS, rhs)),
        in_specs=[whole(), in_hbm()],
        out_specs=(whole(), whole()),
        scratch_shapes=[pltpu.VMEM((TS, BS, BS), jnp.float32), pltpu.SemaphoreType.DMA],
        compiler_params=VMEM,
        name="first",
    )(arrived, diag_stream)
    rights, picks = pl.pallas_call(
        order_kernel,
        out_shape=(
            f32((LEVELS - 1) * TS, BS, rhs),
            jax.ShapeDtypeStruct((2, rows), jnp.int32),
        ),
        in_specs=[whole()],
        out_specs=(whole(), whole()),
        compiler_params=VMEM,
        name="order",
    )(arrived)
    in_smem = pl.BlockSpec(memory_space=pltpu.SMEM)
    leaf = lax.axis_index("leaf")
    at = jnp.stack([lax.axis_index("panel"), leaf // (2 * SIDE), leaf // 2 % SIDE, leaf % 2])
    near = KP * TS * (LEVELS - 1)
    mine = panel_from
    gathered, theirs = gather_core(sent, mine)
    near_tiles = [
        pl.pallas_call(
            functools.partial(near_kernel, which),
            out_shape=b16(near, BS, rhs),
            in_specs=[in_smem] * 3 + [whole()] * 6,
            out_specs=whole(),
            compiler_params=VMEM,
            name=f"near{which}",
        )(at, picks, wanted, *gathered)
        for which, wanted in enumerate((mine, theirs))
    ]
    own, other = near_tiles[0], swap_core(near_tiles[1])
    leaf_right = leaf_noise.reshape(TL, BS, rhs)
    all_solved = [solved]
    offset = 0
    send_offset = 0
    for tree_level in range(LEVELS):
        group = owners >> tree_level
        groups = [
            list(range(g * group, (g + 1) * group)) for g in range(owners // group)
        ]
        if tree_level:
            chosen = send_row[send_offset : send_offset + group]
            buffer = jnp.where((chosen == 0)[:, None, None], sent[0][None], sent[1][None])
            if tree_level == 1:
                gathered, buffer = lax.optimization_barrier((gathered, buffer))
                own_all, other_all = pl.pallas_call(
                    spread_kernel,
                    out_shape=(b16(owners // 2, BS, rhs), b16(owners // 2, BS, rhs)),
                    in_specs=[in_smem] * 2 + [whole()] * 6,
                    out_specs=(whole(), whole()),
                    compiler_params=VMEM,
                    name="spread",
                )(at, picks, *gathered)
                other_all = swap_core(other_all)
            received = lax.all_to_all(
                buffer, AXES, 0, 0, axis_index_groups=groups, tiled=True
            )
        if tree_level == 2:
            leaf_right = leaf_pass(
                functools.partial(top_leaf_kernel, KP * TS * (LEVELS - 1)),
                KP * TS * (LEVELS - 1),
                (panel_from, at),
                (own_all, other_all),
                stream,
                leaf_right,
            )
            leaf_right = leaf_pass(*waiting, leaf_right)
        if tree_level == 3:
            leaf_right = leaf_pass(*waiting, leaf_right)
        if tree_level >= 2:
            received, leaf_right = lax.optimization_barrier((received, leaf_right))
        send_offset += group
        sep_tiles = (LEVELS - 1 - tree_level) * TS
        leaf_offset = offset + KP * sep_tiles
        if tree_level < LEVELS - 1:
            operands = [from_stream, stream, streamed(rights), diag_stream]
            in_specs = [in_hbm()] * 4
            if tree_level:
                kernel = functools.partial(level_kernel, offset, (tree_level + 1) * TS)
                operands.append(received)
                in_specs.append(whole())
                waiting = (
                    functools.partial(leaf_kernel, leaf_offset),
                    leaf_offset,
                    (panel_from,),
                    (received,),
                    stream,
                )
            else:
                kernel = top_kernel
                operands += [at, own, other]
                in_specs += [in_smem, whole(), whole()]
            rights, solved, sent = pl.pallas_call(
                kernel,
                in_specs=in_specs,
                out_specs=(whole(),) * 3,
                out_shape=(
                    f32(max(sep_tiles - TS, TS), BS, rhs),
                    f32(TS, BS, rhs),
                    b16(TS, BS, rhs),
                ),
                scratch_shapes=[
                    pltpu.SMEM(panel_from.shape, jnp.int32),
                    pltpu.VMEM((KP * sep_tiles, BS, BS), jnp.bfloat16),
                    pltpu.VMEM((sep_tiles, BS, rhs), jnp.float32),
                    pltpu.VMEM((TS, BS, BS), jnp.float32),
                    pltpu.SemaphoreType.DMA((4,)),
                ],
                compiler_params=VMEM,
                name=f"level{tree_level}",
            )(*operands)
            all_solved.append(solved)
        else:
            parts = TL // LAST_STEP
            leaf_right = pl.pallas_call(
                functools.partial(last_kernel, leaf_offset),
                in_specs=[in_hbm(), whole()] + [in_hbm()] * 3,
                out_specs=in_hbm(),
                out_shape=pltpu.HBM((TL, BS, rhs), jnp.float32),
                scratch_shapes=[
                    pltpu.SMEM(panel_from.shape, jnp.int32),
                    pltpu.VMEM((KP * TL, BS, BS), jnp.bfloat16),
                    pltpu.VMEM((TL, BS, rhs), jnp.float32),
                    pltpu.VMEM((TL, BS, BS), jnp.float32),
                    pltpu.VMEM((TL, BS, rhs), jnp.float32),
                    pltpu.SemaphoreType.DMA((3 * parts + 1,)),
                    pltpu.SemaphoreType.DMA((parts,)),
                ],
                compiler_params=VMEM,
                name="last",
            )(from_stream, received, stream, streamed(leaf_right), diag_stream)
        offset = leaf_offset + KP * TL
    sep_solution = jnp.concatenate(all_solved, axis=0).reshape(rows, rhs)
    return (sep_solution, leaf_right.reshape(TL * BS, rhs))


def solution(mesh):
    return jax.shard_map(
        per_device,
        mesh=mesh,
        in_specs=(
            P(AXES, None),
            P(AXES),
            P(AXES, None),
            P(AXES, None, None),
            P(AXES, None, None),
            P(AXES),
            P(AXES, None),
        ),
        out_specs=(P(AXES, None), P(AXES, None)),
        check_vma=False,
    )
```

```python
import functools

import jax
import jax.numpy as jnp
from jax import lax
from jax.experimental import pallas as pl
from jax.experimental.pallas import tpu as pltpu
from jax.sharding import PartitionSpec as P

BS = 128
TS = 2
TL = 32
KP = 4
LEVELS = 4
AXES = ("leaf", "panel")
LEAF_STEP = 16
LAST_STEP = 8
SIDE = 4
CUTS = (0, 48, 96, 128)
ORDERS = ("xzy", "zyx", "yxz")
VMEM = pltpu.CompilerParams(vmem_limit_bytes=24 * 1024 * 1024)


def in_hbm():
    return pl.BlockSpec(memory_space=pltpu.HBM)


def whole():
    return pl.BlockSpec(memory_space=pltpu.VMEM)


def halves(x):
    high = x.astype(jnp.bfloat16)
    return high, (x - high.astype(jnp.float32)).astype(jnp.bfloat16)


def hot(condition):
    return condition.astype(jnp.float32).astype(jnp.bfloat16)


def transposed_dot(a, b):
    return lax.dot_general(a, b, (((1,), (1,)), ((), ())), preferred_element_type=jnp.float32)


def pack_kernel(
    target_hbm, send_hbm, noise_hbm, out_ref, target_ref, send_ref, noise_ref, arrived
):
    rows = noise_ref.shape[0]
    owners, per_owner, width = out_ref.shape
    *lists, noise = start(
        (target_hbm, target_ref, arrived.at[0]),
        (send_hbm, send_ref, arrived.at[1]),
        (noise_hbm, noise_ref, arrived.at[2]),
    )
    for copy in lists:
        copy.wait()
    target = target_ref[...]
    owner = target // rows
    slot = target % rows
    mine = owner == lax.broadcasted_iota(jnp.int32, (owners, rows), 0)
    before = lax.broadcasted_iota(jnp.int32, (rows, rows), 0) < lax.broadcasted_iota(
        jnp.int32, (rows, rows), 1
    )
    earlier = jnp.dot(hot(mine), hot(before), preferred_element_type=jnp.float32)
    rank = jnp.sum(jnp.where(mine, earlier, 0.0), axis=0, keepdims=True)
    position = owner * per_owner + rank.astype(jnp.int32)
    select = hot(position == lax.broadcasted_iota(jnp.int32, (rows, rows), 0))
    noise.wait()
    both = jnp.concatenate(halves(noise_ref[...]), axis=1)
    out = jnp.dot(select, both, preferred_element_type=jnp.float32)
    level_rows = TS * BS
    lane = lax.broadcasted_iota(jnp.int32, (BS, rows), 0)
    place = jnp.where(slot // level_rows == lane, slot % level_rows, -1)
    row = lax.broadcasted_iota(jnp.int32, (BS, owners), 0)
    picks = send_ref[:, :owners]
    theirs = (owner ^ SIDE) == lax.broadcasted_iota(jnp.int32, (owners, rows), 0)
    picked = jnp.dot(
        hot((picks > 0) & (row == LEVELS)), hot(mine), preferred_element_type=jnp.float32
    ) + jnp.dot(
        hot((picks > 0) & (row == LEVELS + 1)), hot(theirs), preferred_element_type=jnp.float32
    )
    place = jnp.where(lane < LEVELS, place.astype(jnp.float32), picked)
    meta = transposed_dot(select, place.astype(jnp.bfloat16))
    out = jnp.concatenate([out, meta], axis=1)
    out_ref[...] = out.reshape(owners, per_owner, width).astype(jnp.bfloat16)


def arrived_parts(arrived_ref):
    owners, per_owner, width = arrived_ref.shape
    rows = owners * per_owner
    arrived = arrived_ref[...].astype(jnp.float32).reshape(rows, width).astype(jnp.bfloat16)
    unit = hot(
        lax.broadcasted_iota(jnp.int32, (8, BS), 0) == lax.broadcasted_iota(jnp.int32, (8, BS), 1)
    )
    places = transposed_dot(unit, arrived[:, width - BS :]).astype(jnp.int32)
    return arrived[:, : width - BS], places


def order_rows(arrived, places, tree_level):
    rows, width = arrived.shape
    select = hot(
        places[tree_level : tree_level + 1]
        == lax.broadcasted_iota(jnp.int32, (TS * BS, rows), 0)
    )
    both = jnp.dot(select, arrived, preferred_element_type=jnp.float32)
    return both[:, : width // 2] + both[:, width // 2 :]


def solve(diag, right):
    left = jnp.concatenate(halves(diag), axis=0)
    both = jnp.concatenate(halves(right), axis=1)
    out = jnp.dot(left, both, preferred_element_type=jnp.float32)
    rows, width = diag.shape[0], right.shape[1]
    return (
        out[:rows, :width]
        + (out[:rows, width:] + out[rows:, :width])
        + out[rows:, width:]
    )


def finish(right, diag_ref, t, solved_ref, sent_ref):
    solved = solve(diag_ref[t], right)
    solved_ref[t] = solved
    sent_ref[t] = solved.astype(jnp.bfloat16)


def first_kernel(arrived_ref, diag_hbm, solved_ref, sent_ref, diag_ref, arrived):
    fetch = pltpu.make_async_copy(diag_hbm.at[pl.ds(0, TS)], diag_ref, arrived)
    fetch.start()
    right = order_rows(*arrived_parts(arrived_ref), 0)
    fetch.wait()
    for t in range(TS):
        finish(right[t * BS : (t + 1) * BS], diag_ref, t, solved_ref, sent_ref)


def order_kernel(arrived_ref, out_ref, picks_ref):
    arrived, places = arrived_parts(arrived_ref)
    for i in range(LEVELS - 1):
        right = order_rows(arrived, places, i + 1)
        for t in range(TS):
            out_ref[i * TS + t] = right[t * BS : (t + 1) * BS]
    picks_ref[...] = places[LEVELS : LEVELS + 2]


def step_pairs(axis, second):
    pairs = []
    for device in range(2 * SIDE**3):
        at = {
            "x": device % SIDE,
            "c": device // SIDE % 2,
            "z": device // (2 * SIDE) % SIDE,
            "y": device // (2 * SIDE * SIDE),
        }
        up = (at[axis] + at["c"] + second) % 2 == 0
        at[axis] = (at[axis] + (1 if up else -1)) % SIDE
        pairs.append((device, ((at["y"] * SIDE + at["z"]) * 2 + at["c"]) * SIDE + at["x"]))
    return pairs


def gather_core(sent, early):
    sent, early = lax.optimization_barrier((sent, early))
    parts = [sent[:, a:b] for a, b in zip(CUTS, CUTS[1:])]
    steps = 2 * len(ORDERS[0])
    for step in range(steps):
        arriving = [
            lax.ppermute(part, AXES, step_pairs(order[step // 2], step % 2))
            for part, order in zip(parts, ORDERS)
        ]
        if step == 0:
            early = swap_core(early)
            early, arriving[2] = lax.optimization_barrier((early, arriving[2]))
        if step < steps - 1:
            parts = [
                lax.optimization_barrier(jnp.concatenate(both, axis=0))
                for both in zip(parts, arriving)
            ]
    return [x for both in zip(parts, arriving) for x in both], early


def swap_core(x):
    return lax.ppermute(x, AXES, [(i, i ^ SIDE) for i in range(2 * SIDE**3)])


def same_core(position, at_ref):
    return (position // SIDE) % 2 == at_ref[3]


def take(parts, at_ref, position, pick):
    core = at_ref[3]

    def place(axis, there):
        here = at_ref["xyz".index(axis)]
        away = there - here
        away = jnp.where((here + core) % 2 == 0, away, -away) & (SIDE - 1)
        return away ^ (away >> 1)

    there = {
        "x": position % SIDE,
        "z": position // (2 * SIDE) % SIDE,
        "y": position // (2 * SIDE * SIDE),
    }
    spots = {axis: place(axis, there[axis]) for axis in there}
    for held, came, order in zip(parts[::2], parts[1::2], ORDERS):
        at = 0
        for axis in reversed(order):
            at = at * SIDE + spots[axis]
        at = at * TS + pick
        half = held.shape[0]
        yield jnp.where(at < half, held[at & (half - 1)], came[at & (half - 1)])


def near_kernel(which, at_ref, picks_ref, from_ref, *refs):
    *parts, out_ref = refs
    for e in range(out_ref.shape[0]):
        position = from_ref[e]
        blocks = take(parts, at_ref, position, picks_ref[which, position * 8])
        for first, block in zip(CUTS, blocks):
            out_ref[e, first : first + block.shape[0]] = block


def spread_kernel(at_ref, picks_ref, *refs):
    *parts, own_ref, other_ref = refs

    def body(i, carry):
        position = i // SIDE * (2 * SIDE) + at_ref[3] * SIDE + i % SIDE
        for which, out_ref in enumerate((own_ref, other_ref)):
            blocks = take(parts, at_ref, position, picks_ref[which, position * 8])
            for first, block in zip(CUTS, blocks):
                out_ref[i, first : first + block.shape[0]] = block
        return carry

    lax.fori_loop(0, own_ref.shape[0], body, 0)


def tile_update(panels_ref, local, tile):
    left = jnp.concatenate([panels_ref[local + k] for k in range(KP)], axis=1)
    right = jnp.concatenate([tile(k) for k in range(KP)], axis=0)
    return jnp.dot(left, right, preferred_element_type=jnp.float32)


def start(*pairs):
    copies = [pltpu.make_async_copy(*pair) for pair in pairs]
    for copy in copies:
        copy.start()
    return copies


def load_level(offset, first_diag, sources, targets, arrived):
    from_hbm, panels_hbm, rights_hbm, diag_hbm = sources
    from_ref, panels_ref, rights_ref, diag_ref = targets
    copies = start(
        (from_hbm, from_ref, arrived.at[0]),
        (panels_hbm.at[pl.ds(offset, panels_ref.shape[0])], panels_ref, arrived.at[1]),
        (rights_hbm, rights_ref, arrived.at[2]),
        (diag_hbm.at[pl.ds(first_diag, TS)], diag_ref, arrived.at[3]),
    )
    for copy in copies:
        copy.wait()


def run_level(tile, panels_ref, rights_ref, diag_ref, rest_ref, solved_ref, sent_ref):
    for d in range(rights_ref.shape[0]):
        right = rights_ref[d] - tile_update(panels_ref, KP * d, lambda k: tile(KP * d + k))
        if d < TS:
            finish(right, diag_ref, d, solved_ref, sent_ref)
        else:
            rest_ref[d - TS] = right


def level_kernel(
    offset, first_diag, from_hbm, panels_hbm, rights_hbm, diag_hbm, received_ref,
    rest_ref, solved_ref, sent_ref, from_ref, panels_ref, rights_ref, diag_ref, arrived,
):
    load_level(
        offset, first_diag, (from_hbm, panels_hbm, rights_hbm, diag_hbm),
        (from_ref, panels_ref, rights_ref, diag_ref), arrived,
    )
    run_level(
        lambda e: received_ref[from_ref[offset + e]],
        panels_ref, rights_ref, diag_ref, rest_ref, solved_ref, sent_ref,
    )


def top_kernel(
    from_hbm, panels_hbm, rights_hbm, diag_hbm, at_ref, own_ref, other_ref,
    rest_ref, solved_ref, sent_ref, from_ref, panels_ref, rights_ref, diag_ref, arrived,
):
    load_level(
        0, TS, (from_hbm, panels_hbm, rights_hbm, diag_hbm),
        (from_ref, panels_ref, rights_ref, diag_ref), arrived,
    )
    run_level(
        lambda e: jnp.where(same_core(from_ref[e], at_ref), own_ref[e], other_ref[e]),
        panels_ref, rights_ref, diag_ref, rest_ref, solved_ref, sent_ref,
    )


def top_leaf_kernel(offset, from_ref, at_ref, own_ref, other_ref, panels_ref, right_ref, out_ref):
    first = offset + pl.program_id(0) * LEAF_STEP * KP

    def tile(entry):
        position = from_ref[entry]
        slot = position // (2 * SIDE) * SIDE + position % SIDE
        return jnp.where(same_core(position, at_ref), own_ref[slot], other_ref[slot])

    for d in range(LEAF_STEP):
        out_ref[d] = right_ref[d] - tile_update(
            panels_ref, KP * d, lambda k: tile(first + KP * d + k)
        )


def leaf_kernel(offset, from_ref, received_ref, panels_ref, right_ref, out_ref):
    first = offset + pl.program_id(0) * LEAF_STEP * KP
    for d in range(LEAF_STEP):
        out_ref[d] = right_ref[d] - tile_update(
            panels_ref, KP * d, lambda k: received_ref[from_ref[first + KP * d + k]]
        )


def last_kernel(
    offset, from_hbm, received_ref, panels_hbm, right_hbm, diag_hbm, out_hbm,
    from_ref, panels_ref, right_ref, diag_ref, out_ref, arrived, left,
):
    parts = TL // LAST_STEP
    [chosen] = start((from_hbm, from_ref, arrived.at[3 * parts]))
    loads = []
    for part in range(parts):
        first = part * LAST_STEP
        tiles = pl.ds(first, LAST_STEP)
        entries = pl.ds(KP * first, KP * LAST_STEP)
        loads.append(
            start(
                (
                    panels_hbm.at[pl.ds(offset + KP * first, KP * LAST_STEP)],
                    panels_ref.at[entries],
                    arrived.at[3 * part],
                ),
                (right_hbm.at[tiles], right_ref.at[tiles], arrived.at[3 * part + 1]),
                (
                    diag_hbm.at[pl.ds(LEVELS * TS + first, LAST_STEP)],
                    diag_ref.at[tiles],
                    arrived.at[3 * part + 2],
                ),
            )
        )
    chosen.wait()
    stores = []
    for part in range(parts):
        for copy in loads[part]:
            copy.wait()
        tiles = range(part * LAST_STEP, (part + 1) * LAST_STEP)
        rights = [
            right_ref[t]
            - tile_update(
                panels_ref, KP * t, lambda k: received_ref[from_ref[offset + KP * t + k]]
            )
            for t in tiles
        ]
        for t, right in zip(tiles, rights):
            out_ref[t] = solve(diag_ref[t], right)
        done = pl.ds(part * LAST_STEP, LAST_STEP)
        stores += start((out_ref.at[done], out_hbm.at[done], left.at[part]))
    for copy in stores:
        copy.wait()


def entries_block(offset, count):
    return pl.BlockSpec(
        (pl.Element(count), pl.Element(BS), pl.Element(BS)),
        lambda i, *_: (offset + i * count, 0, 0),
    )


def streamed(x):
    return pltpu.with_memory_space_constraint(x, pltpu.HBM)


def f32(*shape):
    return jax.ShapeDtypeStruct(shape, jnp.float32)


def b16(*shape):
    return jax.ShapeDtypeStruct(shape, jnp.bfloat16)


def leaf_pass(kernel, offset, scalars, received, stream, leaf_right):
    tiles, rows, rhs = leaf_right.shape
    return pl.pallas_call(
        kernel,
        grid_spec=pltpu.PrefetchScalarGridSpec(
            num_scalar_prefetch=len(scalars),
            grid=(tiles // LEAF_STEP,),
            in_specs=[whole()] * len(received)
            + [entries_block(offset, KP * LEAF_STEP), entries_block(0, LEAF_STEP)],
            out_specs=entries_block(0, LEAF_STEP),
        ),
        out_shape=pltpu.HBM((tiles, rows, rhs), jnp.float32),
        compiler_params=VMEM,
        name="leaf",
    )(*scalars, *received, stream, streamed(leaf_right))


def per_device(
    noise_parts, elimination_row, leaf_noise, diag_inverse, panels, panel_from, send_lists
):
    owners = lax.axis_size(AXES)
    rows = noise_parts.shape[0]
    rhs = noise_parts.shape[1]
    per_owner = rows // owners
    outgoing = pl.pallas_call(
        pack_kernel,
        out_shape=b16(owners, per_owner, 2 * rhs + BS),
        in_specs=[in_hbm()] * 3,
        out_specs=whole(),
        scratch_shapes=[
            pltpu.VMEM((1, rows), jnp.int32),
            pltpu.VMEM(send_lists.shape, jnp.int32),
            pltpu.VMEM((rows, rhs), jnp.float32),
            pltpu.SemaphoreType.DMA((3,)),
        ],
        compiler_params=VMEM,
        name="pack",
    )(*map(streamed, (elimination_row.reshape(1, rows), send_lists, noise_parts)))
    arrived = lax.all_to_all(outgoing, AXES, 0, 0, tiled=True)
    send_row = send_lists[0]
    stream = streamed(panels)
    diag_stream = streamed(diag_inverse)
    from_stream = streamed(panel_from)
    solved, sent = pl.pallas_call(
        first_kernel,
        out_shape=(f32(TS, BS, rhs), b16(TS, BS, rhs)),
        in_specs=[whole(), in_hbm()],
        out_specs=(whole(), whole()),
        scratch_shapes=[pltpu.VMEM((TS, BS, BS), jnp.float32), pltpu.SemaphoreType.DMA],
        compiler_params=VMEM,
        name="first",
    )(arrived, diag_stream)
    rights, picks = pl.pallas_call(
        order_kernel,
        out_shape=(
            f32((LEVELS - 1) * TS, BS, rhs),
            jax.ShapeDtypeStruct((2, rows), jnp.int32),
        ),
        in_specs=[whole()],
        out_specs=(whole(), whole()),
        compiler_params=VMEM,
        name="order",
    )(arrived)
    in_smem = pl.BlockSpec(memory_space=pltpu.SMEM)
    leaf = lax.axis_index("leaf")
    at = jnp.stack([lax.axis_index("panel"), leaf // (2 * SIDE), leaf // 2 % SIDE, leaf % 2])
    near = KP * TS * (LEVELS - 1)
    mine = panel_from
    gathered, theirs = gather_core(sent, mine)
    near_tiles = [
        pl.pallas_call(
            functools.partial(near_kernel, which),
            out_shape=b16(near, BS, rhs),
            in_specs=[in_smem] * 3 + [whole()] * 6,
            out_specs=whole(),
            compiler_params=VMEM,
            name=f"near{which}",
        )(at, picks, wanted, *gathered)
        for which, wanted in enumerate((mine, theirs))
    ]
    own, other = near_tiles[0], swap_core(near_tiles[1])
    leaf_right = leaf_noise.reshape(TL, BS, rhs)
    all_solved = [solved]
    offset = 0
    send_offset = 0
    for tree_level in range(LEVELS):
        group = owners >> tree_level
        groups = [
            list(range(g * group, (g + 1) * group)) for g in range(owners // group)
        ]
        if tree_level:
            chosen = send_row[send_offset : send_offset + group]
            buffer = jnp.where((chosen == 0)[:, None, None], sent[0][None], sent[1][None])
            if tree_level == 1:
                gathered, buffer = lax.optimization_barrier((gathered, buffer))
                own_all, other_all = pl.pallas_call(
                    spread_kernel,
                    out_shape=(b16(owners // 2, BS, rhs), b16(owners // 2, BS, rhs)),
                    in_specs=[in_smem] * 2 + [whole()] * 6,
                    out_specs=(whole(), whole()),
                    compiler_params=VMEM,
                    name="spread",
                )(at, picks, *gathered)
                other_all = swap_core(other_all)
            received = lax.all_to_all(
                buffer, AXES, 0, 0, axis_index_groups=groups, tiled=True
            )
        if tree_level == 2:
            leaf_right = leaf_pass(
                functools.partial(top_leaf_kernel, KP * TS * (LEVELS - 1)),
                KP * TS * (LEVELS - 1),
                (panel_from, at),
                (own_all, other_all),
                stream,
                leaf_right,
            )
            leaf_right = leaf_pass(*waiting, leaf_right)
        if tree_level == 3:
            leaf_right = leaf_pass(*waiting, leaf_right)
        if tree_level >= 2:
            received, leaf_right = lax.optimization_barrier((received, leaf_right))
        send_offset += group
        sep_tiles = (LEVELS - 1 - tree_level) * TS
        leaf_offset = offset + KP * sep_tiles
        if tree_level < LEVELS - 1:
            operands = [from_stream, stream, streamed(rights), diag_stream]
            in_specs = [in_hbm()] * 4
            if tree_level:
                kernel = functools.partial(level_kernel, offset, (tree_level + 1) * TS)
                operands.append(received)
                in_specs.append(whole())
                waiting = (
                    functools.partial(leaf_kernel, leaf_offset),
                    leaf_offset,
                    (panel_from,),
                    (received,),
                    stream,
                )
            else:
                kernel = top_kernel
                operands += [at, own, other]
                in_specs += [in_smem, whole(), whole()]
            rights, solved, sent = pl.pallas_call(
                kernel,
                in_specs=in_specs,
                out_specs=(whole(),) * 3,
                out_shape=(
                    f32(max(sep_tiles - TS, TS), BS, rhs),
                    f32(TS, BS, rhs),
                    b16(TS, BS, rhs),
                ),
                scratch_shapes=[
                    pltpu.SMEM(panel_from.shape, jnp.int32),
                    pltpu.VMEM((KP * sep_tiles, BS, BS), jnp.bfloat16),
                    pltpu.VMEM((sep_tiles, BS, rhs), jnp.float32),
                    pltpu.VMEM((TS, BS, BS), jnp.float32),
                    pltpu.SemaphoreType.DMA((4,)),
                ],
                compiler_params=VMEM,
                name=f"level{tree_level}",
            )(*operands)
            all_solved.append(solved)
        else:
            parts = TL // LAST_STEP
            leaf_right = pl.pallas_call(
                functools.partial(last_kernel, leaf_offset),
                in_specs=[in_hbm(), whole()] + [in_hbm()] * 3,
                out_specs=in_hbm(),
                out_shape=pltpu.HBM((TL, BS, rhs), jnp.float32),
                scratch_shapes=[
                    pltpu.SMEM(panel_from.shape, jnp.int32),
                    pltpu.VMEM((KP * TL, BS, BS), jnp.bfloat16),
                    pltpu.VMEM((TL, BS, rhs), jnp.float32),
                    pltpu.VMEM((TL, BS, BS), jnp.float32),
                    pltpu.VMEM((TL, BS, rhs), jnp.float32),
                    pltpu.SemaphoreType.DMA((3 * parts + 1,)),
                    pltpu.SemaphoreType.DMA((parts,)),
                ],
                compiler_params=VMEM,
                name="last",
            )(from_stream, received, stream, streamed(leaf_right), diag_stream)
        offset = leaf_offset + KP * TL
    sep_solution = jnp.concatenate(all_solved, axis=0).reshape(rows, rhs)
    return (sep_solution, leaf_right.reshape(TL * BS, rhs))


def solution(mesh):
    return jax.shard_map(
        per_device,
        mesh=mesh,
        in_specs=(
            P(AXES, None),
            P(AXES),
            P(AXES, None),
            P(AXES, None, None),
            P(AXES, None, None),
            P(AXES),
            P(AXES, None),
        ),
        out_specs=(P(AXES, None), P(AXES, None)),
        check_vma=False,
    )
```
